512 devices in a mesh: ctx: 64 (over z, x), head: 8 (over y, core).
Axes of the slice: x: 4, y: 4, z: 16, core: 2. Of those that a mesh axis runs over, the one named last changes fastest.
Arguments:
- values: float32 [8192, 4096], P('ctx', 'head'), may hold values from -6 to 6
- step_size: float32 [64, 8192], P('head', 'ctx'), may hold values from 7.6293945e-07 to 0.52, as said below
- decay_rate: float32 [64], P('head'), may hold values from -4 to -1, as said below
- input_map: float32 [8192, 128], P('ctx'), may hold values from -3 to 3
- output_map: float32 [8192, 128], P('ctx'), may hold values from -3 to 3
- skip_gain: float32 [64], P('head'), may hold values from 0.5 to 1.5
- grad_output: float32 [8192, 4096], P('ctx', 'head'), may hold values from -6 to 6
Outputs:
- outputs: float32 [8192, 4096], P('ctx', 'head')
- grad_values: float32 [8192, 4096], P('ctx', 'head')
- grad_input_map: float32 [8192, 128], P(('ctx', 'head'))
- grad_output_map: float32 [8192, 128], P(('ctx', 'head'))
The draws below stay inside these ranges and needn't reach their ends.
Inputs may be any that keep to these rules, and one draw needn't show every extreme that they name: `step_size`: step sizes, each positive. `decay_rate`: decay rates, each negative.
All inputs are finite; a program needn't handle non-finite values.
Results may differ from the reference program's by a relative error of at most 0.0003.
Values sent between devices are 32-bit elements; how exact they have to be, the bound alone decides.
A program may use at most 128 MiB of HBM per device.

```python
import math
import jax
import jax.numpy as jnp
from jax import lax

HEAD_TOTAL = 64
HEAD_DIM = 64
STATE = 128
GROUP = 128
TOK_DEV = 128
TOKEN_TOTAL = 8192


def decay_magnitude(key):
    return jax.random.uniform(key, (HEAD_TOTAL,), jnp.float32, 1.0, 4.0)


def draw_decay_rate(key, part):
    return -decay_magnitude(key)


def draw_step_size(key, part):
    absolute_level = decay_magnitude(key)
    key = jax.random.fold_in(key, 7)
    key_sequence = jax.random.split(key, 7)
    slow_share = 0.5
    slow_heads = jax.random.uniform(key_sequence[0], (HEAD_TOTAL,), jnp.float32) < slow_share
    fast_rate = jax.random.uniform(key_sequence[1], (HEAD_TOTAL,), jnp.float32, 1.0 / 50.0, 1.0 / 30.0)
    slow_rate = jax.random.uniform(key_sequence[2], (HEAD_TOTAL,), jnp.float32, 0.1, 0.6) / TOKEN_TOTAL
    head_rate = jnp.where(slow_heads, slow_rate, fast_rate)
    spread = math.log(2.0)
    roughness = jnp.exp(jax.random.uniform(key_sequence[3], (HEAD_TOTAL, TOKEN_TOTAL), jnp.float32, -spread, spread))
    device_factor = jnp.exp(jax.random.uniform(key_sequence[4], (HEAD_TOTAL, TOKEN_TOTAL // TOK_DEV), jnp.float32, -spread, spread))
    device_factor = jnp.repeat(device_factor, TOK_DEV, axis=1)
    baseline_widths = (head_rate / absolute_level)[:, None] * roughness * device_factor
    spike_mask = jax.random.uniform(key_sequence[5], (HEAD_TOTAL, TOKEN_TOTAL), jnp.float32) < 3.0 / TOKEN_TOTAL
    retained_fraction = jax.random.uniform(key_sequence[6], (HEAD_TOTAL, TOKEN_TOTAL), jnp.float32, 0.6, 0.8)
    increment_widths = jnp.where(spike_mask, -jnp.log(retained_fraction) / absolute_level[:, None], baseline_widths)
    return jnp.clip(increment_widths, 0.00625 / TOKEN_TOTAL, 0.52)


def block_scale(rng, shape, cuts, least, top_value):
    gain, own = 1.0, jax.random.fold_in(rng, 6)
    for axis_at, blocks in cuts:
        heights = jnp.exp(jax.random.uniform(jax.random.fold_in(own, axis_at), (blocks,), jnp.float32, least / len(cuts), top_value / len(cuts)))
        gain = gain * jnp.repeat(heights, shape[axis_at] // blocks).reshape([-1 if axis == axis_at else 1 for axis in range(len(shape))])
    return gain


def normal_values(key, extent, width, bound, pieces=(), kind=jnp.bfloat16):
    entries = width * jax.random.normal(key, extent, jnp.float32)
    if pieces:
        entries = entries * block_scale(key, extent, pieces, -0.22, 0.18)
    return jnp.clip(entries, -bound, bound).astype(kind)


def setup_inputs(seed: int = 0) -> dict:
    arg_keys = jax.random.split(jax.random.key(seed), 8)
    return {
        "values": normal_values(arg_keys[0], (TOKEN_TOTAL, HEAD_TOTAL * HEAD_DIM), 1.0, 6.0, ((0, 64), (1, 8)), jnp.float32),
        "step_size": draw_step_size(jax.random.fold_in(arg_keys[7], 71), 0),
        "decay_rate": draw_decay_rate(jax.random.fold_in(arg_keys[7], 71), 0),
        "input_map": normal_values(arg_keys[3], (TOKEN_TOTAL, STATE), 0.5, 3.0, ((0, 64),), jnp.float32),
        "output_map": normal_values(arg_keys[4], (TOKEN_TOTAL, STATE), 0.5, 3.0, ((0, 64),), jnp.float32),
        "skip_gain": jnp.clip(0.5 + 1.0 * jax.random.uniform(arg_keys[5], (HEAD_TOTAL,), jnp.float32) ** block_scale(arg_keys[5], (HEAD_TOTAL,), ((0, 8),), -0.2, 0.2), 0.5, 1.5),
        "grad_output": normal_values(arg_keys[6], (TOKEN_TOTAL, HEAD_TOTAL * HEAD_DIM), 1.0, 6.0, ((0, 64), (1, 8)), jnp.float32),
    }


PRECISE = lax.Precision.HIGHEST


def block_parts(step_block, input_block, output_block, value_block, grad_block, decay_rate):
    cumulative = jnp.cumsum(step_block * decay_rate[:, None], axis=1)
    causal = jnp.arange(GROUP)[:, None] >= jnp.arange(GROUP)[None, :]
    gaps = cumulative[:, :, None] - cumulative[:, None, :]
    decay = jnp.where(causal[None], jnp.exp(jnp.where(causal[None], gaps, 0.0)), 0.0)
    scores = jnp.einsum("tn,sn->ts", output_block, input_block, precision=PRECISE)
    weighted = scores[None] * decay
    scaled = value_block * step_block.T[:, :, None]
    intersections = jnp.einsum("thp,shp->hts", grad_block, scaled, precision=PRECISE) * decay
    totals = cumulative[:, -1]
    to_end = jnp.exp(totals[:, None] - cumulative)
    from_start = jnp.exp(cumulative)
    return weighted, scaled, intersections, to_end, from_start, totals


def reference(values, step_size, decay_rate, input_map, output_map, skip_gain, grad_output):
    block_count = TOKEN_TOTAL // GROUP
    head_width = values.shape[1] // HEAD_TOTAL
    value_blocks = values.reshape(block_count, GROUP, HEAD_TOTAL, head_width)
    grad_blocks = grad_output.reshape(block_count, GROUP, HEAD_TOTAL, head_width)
    step_blocks = step_size.reshape(HEAD_TOTAL, block_count, GROUP).transpose(1, 0, 2)
    input_blocks = input_map.reshape(block_count, GROUP, STATE)
    output_blocks = output_map.reshape(block_count, GROUP, STATE)
    all_blocks = (step_blocks, input_blocks, output_blocks, value_blocks, grad_blocks)

    def forward_step(carry_state, block):
        step_block, input_block, output_block, value_block, grad_block = block
        weighted, scaled, intersections, to_end, from_start, totals = block_parts(step_block, input_block, output_block, value_block, grad_block, decay_rate)
        block_out = jnp.einsum("hts,shp->thp", weighted, scaled, precision=PRECISE)
        block_out = block_out + from_start.T[:, :, None] * jnp.einsum("tn,hnp->thp", output_block, carry_state, precision=PRECISE)
        block_out = block_out + skip_gain[None, :, None] * value_block
        output_grad = jnp.einsum("hts,sn->tn", intersections, input_block, precision=PRECISE)
        output_grad = output_grad + jnp.einsum("ht,hnp,thp->tn", from_start, carry_state, grad_block, precision=PRECISE)
        next_state = jnp.exp(totals)[:, None, None] * carry_state + jnp.einsum("ht,tn,thp->hnp", to_end, input_block, scaled, precision=PRECISE)
        return next_state, (block_out, output_grad)

    def backward_step(later_state, block):
        step_block, input_block, output_block, value_block, grad_block = block
        weighted, scaled, intersections, to_end, from_start, totals = block_parts(step_block, input_block, output_block, value_block, grad_block, decay_rate)
        values_grad = jnp.einsum("hst,shp->thp", weighted, grad_block, precision=PRECISE)
        values_grad = values_grad + to_end.T[:, :, None] * jnp.einsum("tn,hnp->thp", input_block, later_state, precision=PRECISE)
        values_grad = step_block.T[:, :, None] * values_grad + skip_gain[None, :, None] * grad_block
        input_grad = jnp.einsum("hts,tn->sn", intersections, output_block, precision=PRECISE)
        input_grad = input_grad + jnp.einsum("ht,hnp,thp->tn", to_end, later_state, scaled, precision=PRECISE)
        next_later = jnp.exp(totals)[:, None, None] * later_state + jnp.einsum("ht,tn,thp->hnp", from_start, output_block, grad_block, precision=PRECISE)
        return next_later, (values_grad, input_grad)

    zero_state = jnp.zeros((HEAD_TOTAL, STATE, head_width), jnp.float32)
    unused, (block_outputs, output_grads) = lax.scan(forward_step, zero_state, all_blocks)
    unused_later, (values_grads, input_grads) = lax.scan(backward_step, zero_state, all_blocks, reverse=True)
    return (block_outputs.reshape(TOKEN_TOTAL, HEAD_TOTAL * head_width), values_grads.reshape(TOKEN_TOTAL, HEAD_TOTAL * head_width), input_grads.reshape(TOKEN_TOTAL, STATE), output_grads.reshape(TOKEN_TOTAL, STATE))
```

```python
import functools

import jax
import jax.numpy as jnp
from jax import lax
from jax.experimental import pallas as pl
from jax.experimental.pallas import tpu as pltpu
from jax.sharding import PartitionSpec as P

MESH = pl.DeviceIdType.MESH
F32, BF16 = jnp.float32, jnp.bfloat16
NX, NZ, NH = 4, 16, 8
FAR_Z = (8, 7, 9, 6, 10, 5, 11, 4, 12, 3, 13, 2, 14, 1, 15)
FAR_X = (2, 1, 3)
FAR_H = (4, 5, 3, 6, 2, 7, 1)
NN = (((1,), (0,)), ((), ()))
NT = (((1,), (1,)), ((), ()))


def split(x):
    high = x.astype(BF16)
    return high, (x - high.astype(F32)).astype(BF16)


def dot3(a, b, dims=NN):
    (ah, al), (bh, bl) = a, b
    one = functools.partial(lax.dot_general, dimension_numbers=dims, preferred_element_type=F32)
    return one(ah, bh) + (one(al, bh) + one(ah, bl))


def core_kernel(
    v_hbm, step_hbm, rate, b_hbm, c_hbm, gain, g_hbm,
    out_hbm, gv_hbm, maps_out,
    v, g, step, bmap, cmap,
    out_acc, gv_acc, from_w, end_w, gf_h, gf_l, xe_h, xe_l, local_maps,
    xs_f, xs_b, xr_f, xr_b, zs_f, zs_b, zr_f, zr_b, ys_f, ys_b, enter, leave, ws_f, ws_b, inc, fol, rs_s, rs_r,
    load_sem, x1_s, x1_r, z1_s, z1_r, z2_s, z2_r, x2_s, x2_r, rs_ss, rs_rs, out_sem,
):
    ctx, head = lax.axis_index("ctx"), lax.axis_index("head")
    mz, mx = ctx // NX, ctx % NX

    def at_x(d):
        return (mz * NX + lax.rem(mx + d, NX), head)

    def at_z(d):
        return (lax.rem(mz + d, NZ) * NX + mx, head)

    def at_h(d):
        return (ctx, lax.rem(head + d, NH))

    barrier = pltpu.get_barrier_semaphore()
    partners = [at_z(d) for d in FAR_Z] + [at_h(d) for d in FAR_H] + [at_x(d) for d in FAR_X]
    for partner in partners:
        pl.semaphore_signal(barrier, inc=1, device_id=partner, device_id_type=MESH)

    loads = [
        pltpu.make_async_copy(src, dst, load_sem.at[i])
        for i, (src, dst) in enumerate(
            ((step_hbm, step), (b_hbm, bmap), (c_hbm, cmap), (v_hbm, v), (g_hbm, g))
        )
    ]
    for load in loads:
        load.start()

    rows = lax.broadcasted_iota(jnp.int32, (128, 128), 0)
    lanes = lax.broadcasted_iota(jnp.int32, (128, 128), 1)
    first = lanes < 64
    lower = rows >= lanes
    upper = rows <= lanes

    loads[0].wait()
    steps = step[...]
    head_rows = lax.broadcasted_iota(jnp.int32, (NH, 128), 0)
    rates = jnp.zeros((NH, 128), F32)
    for h in range(NH):
        rates = jnp.where(head_rows == h, rate[h], rates)
    cum = lax.dot_general(
        steps * rates, jnp.where(upper, 1.0, 0.0).astype(F32), NN,
        precision=lax.Precision.HIGHEST, preferred_element_type=F32,
    )
    total = cum[:, 127:128]
    table = jnp.concatenate([steps, jnp.exp(cum), jnp.exp(total - cum), cum] + [jnp.zeros((96, 128), F32)], axis=0)
    table = table.T

    def column(kind, h):
        k = kind * NH + h
        return jnp.broadcast_to(table[:, k : k + 1], (128, 128))

    def pair(kind, q):
        return jnp.where(first, column(kind, 2 * q), column(kind, 2 * q + 1))

    loads[1].wait()
    loads[2].wait()
    b_all, c_all = bmap[...], cmap[...]
    b2, c2 = split(b_all), split(c_all)
    bt2, ct2 = split(b_all.T), split(c_all.T)
    loads[3].wait()
    loads[4].wait()

    scaled = []
    for q in range(NX):
        cols = slice(q * 128, (q + 1) * 128)
        step_w, start, end = pair(0, q), pair(1, q), pair(2, q)
        vq, gq = v[:, cols], g[:, cols]
        x = vq * step_w
        scaled.append(x)
        xe, gf = split(x * end), split(gq * start)
        xe_h[q], xe_l[q] = xe
        gf_h[q], gf_l[q] = gf
        from_w[q] = start
        end_w[q] = end * step_w
        xs_f[q, 0:128, :] = dot3(bt2, xe)
        xs_f[q, 128:129, :] = start[127:128, :]
        xs_b[q] = dot3(ct2, gf)

    scores, scores_t = dot3(c2, b2, NT), dot3(b2, c2, NT)
    inner = jnp.zeros((128, 128), F32)
    for q in range(NX):
        cols = slice(q * 128, (q + 1) * 128)
        x, gq = scaled[q], g[:, cols]
        x2, g2 = split(x), split(gq)
        outs, grads = [], []
        for k in range(2):
            h = 2 * q + k
            mine = first if k == 0 else jnp.logical_not(first)
            gap = column(3, h) - cum[h : h + 1, :]
            decay = jnp.exp(jnp.where(lower, gap, -gap))
            below = jnp.where(lower, decay, 0.0)
            above = jnp.where(upper, decay, 0.0)
            part = split(jnp.where(mine, gq, 0.0))
            inner = inner + dot3(part, x2, NT) * below
            outs.append(dot3(split(scores * below), x2))
            grads.append(dot3(split(scores_t * above), g2))
        skip = jnp.where(first[0:1], gain[2 * q], gain[2 * q + 1])
        step_w = pair(0, q)
        out_acc[q] = jnp.where(first, outs[0], outs[1]) + skip * v[:, cols]
        gv_acc[q] = step_w * jnp.where(first, grads[0], grads[1]) + skip * gq
    local_maps[0] = dot3(split(inner), b2)
    local_maps[1] = dot3(split(inner.T), c2)

    pl.semaphore_wait(barrier, len(partners))

    def send(src, dst, send_sem, recv_sem, partner):
        copy = pltpu.make_async_remote_copy(
            src_ref=src, dst_ref=dst, send_sem=send_sem, recv_sem=recv_sem, device_id=partner, device_id_type=MESH
        )
        copy.start()
        return copy

    sent = []

    x1 = []
    for i, (source, target) in enumerate(((xs_f, xr_f), (xs_b, xr_b))):
        x1.append([
            send(source.at[lax.rem(mx + d, NX)], target.at[mx], x1_s.at[i, d - 1], x1_r.at[i, d - 1], at_x(d))
            for d in FAR_X
        ])
        target[mx] = source[mx]
    sent += x1[0] + x1[1]

    z1 = []
    for copy in x1[0]:
        copy.wait_recv()
    decays = [xr_f[k, 128:129, :] for k in range(NX)]
    acc = xr_f[0, 0:128, :]
    for k in range(1, NX):
        acc = acc * decays[k] + xr_f[k, 0:128, :]
    plane = decays[0] * decays[1] * decays[2] * decays[3]
    for j in range(NZ):
        zs_f[j, 0:8, :] = acc[8 * j : 8 * j + 8, :]
        zs_f[j, 8:9, :] = plane
    z1.append([
        send(zs_f.at[lax.rem(mz + d, NZ)], zr_f.at[mz], z1_s.at[0, d - 1], z1_r.at[0, d - 1], at_z(d)) for d in FAR_Z
    ])
    zr_f[mz] = zs_f[mz]
    for copy in x1[1]:
        copy.wait_recv()
    acc = xr_b[NX - 1]
    for k in range(NX - 2, -1, -1):
        acc = acc * decays[k] + xr_b[k]
    for j in range(NZ):
        zs_b[j] = acc[8 * j : 8 * j + 8, :]
    z1.append([
        send(zs_b.at[lax.rem(mz + d, NZ)], zr_b.at[mz], z1_s.at[1, d - 1], z1_r.at[1, d - 1], at_z(d)) for d in FAR_Z
    ])
    zr_b[mz] = zs_b[mz]
    sent += z1[0] + z1[1]

    z2 = []
    mine_rows = pl.ds(pl.multiple_of(mz * 8, 8), 8)
    for copy in z1[0]:
        copy.wait_recv()
    carry = jnp.zeros((8, 128), F32)
    for j in range(NZ):
        ys_f[j] = carry
        carry = carry * zr_f[j, 8:9, :] + zr_f[j, 0:8, :]
    z2.append([
        send(ys_f.at[lax.rem(mz + d, NZ)], enter.at[mine_rows], z2_s.at[0, d - 1], z2_r.at[0, d - 1], at_z(d))
        for d in FAR_Z
    ])
    enter[mine_rows, :] = ys_f[mz]
    for copy in z1[1]:
        copy.wait_recv()
    carry = jnp.zeros((8, 128), F32)
    for j in range(NZ - 1, -1, -1):
        ys_b[j] = carry
        carry = carry * zr_f[j, 8:9, :] + zr_b[j]
    z2.append([
        send(ys_b.at[lax.rem(mz + d, NZ)], leave.at[mine_rows], z2_s.at[1, d - 1], z2_r.at[1, d - 1], at_z(d))
        for d in FAR_Z
    ])
    leave[mine_rows, :] = ys_b[mz]
    sent += z2[0] + z2[1]

    x2 = []
    for copy in z2[0]:
        copy.wait_recv()
    carry = enter[...]
    for k in range(NX):
        ws_f[k] = carry
        if k < NX - 1:
            carry = carry * decays[k] + xr_f[k, 0:128, :]
    x2.append([
        send(ws_f.at[lax.rem(mx + d, NX)], inc.at[mx], x2_s.at[0, d - 1], x2_r.at[0, d - 1], at_x(d)) for d in FAR_X
    ])
    inc[mx] = ws_f[mx]
    for copy in z2[1]:
        copy.wait_recv()
    carry = leave[...]
    for k in range(NX - 1, -1, -1):
        ws_b[k] = carry
        if k > 0:
            carry = carry * decays[k] + xr_b[k]
    x2.append([
        send(ws_b.at[lax.rem(mx + d, NX)], fol.at[mx], x2_s.at[1, d - 1], x2_r.at[1, d - 1], at_x(d)) for d in FAR_X
    ])
    fol[mx] = ws_b[mx]
    sent += x2[0] + x2[1]

    rs, stores = [], []
    plans = (
        (inc, c2, gf_h, gf_l, from_w, out_acc, out_hbm),
        (fol, b2, xe_h, xe_l, end_w, gv_acc, gv_hbm),
    )
    for i, (carried, map2, w_h, w_l, weight, acc_ref, hbm) in enumerate(plans):
        for copy in x2[i]:
            copy.wait_recv()
        grad = local_maps[i]
        for q in range(NX):
            state2 = split(carried[q])
            acc_ref[q] = acc_ref[q] + weight[q] * dot3(map2, state2)
            grad = grad + dot3((w_h[q], w_l[q]), state2, NT)
            store = pltpu.make_async_copy(acc_ref.at[q], hbm.at[:, pl.ds(q * 128, 128)], out_sem.at[i, q])
            store.start()
            stores.append(store)
        for k in range(NH):
            rs_s[i, k] = grad[16 * k : 16 * k + 16, :]
        rs.append([
            send(rs_s.at[i, lax.rem(head + d, NH)], rs_r.at[i, head], rs_ss.at[i, d - 1], rs_rs.at[i, d - 1], at_h(d))
            for d in FAR_H
        ])
        rs_r[i, head] = rs_s[i, head]
    sent += rs[0] + rs[1]
    for i in range(2):
        for copy in rs[i]:
            copy.wait_recv()
        whole = rs_r[i, 0]
        for k in range(1, NH):
            whole = whole + rs_r[i, k]
        maps_out[i] = whole
    for copy in stores:
        copy.wait()
    for copy in sent:
        copy.wait_send()


def hand_kernel(out_in, gv_in, maps_in, out, gv, gi, go, sem):
    copies = [
        pltpu.make_async_copy(src, dst, sem.at[i])
        for i, (src, dst) in enumerate(((out_in, out), (gv_in, gv), (maps_in.at[1], gi), (maps_in.at[0], go)))
    ]
    for copy in copies:
        copy.start()
    for copy in copies:
        copy.wait()


def shards(values, step_size, decay_rate, input_map, output_map, skip_gain, grad_output):
    anywhere = pl.BlockSpec(memory_space=pl.ANY)
    scalars = pl.BlockSpec(memory_space=pltpu.SMEM)
    vmem = lambda *shape, dtype=F32: pltpu.VMEM(shape, dtype)
    dma = lambda *shape: pltpu.SemaphoreType.DMA(shape)
    full = jax.ShapeDtypeStruct(values.shape, F32)
    out, gv, maps = pl.pallas_call(
        core_kernel,
        name="scan_core",
        out_shape=(full, full, jax.ShapeDtypeStruct((2, 16, 128), F32)),
        in_specs=[anywhere, anywhere, scalars, anywhere, anywhere, scalars, anywhere],
        out_specs=(anywhere, anywhere, pl.BlockSpec(memory_space=pltpu.VMEM)),
        scratch_shapes=[
            vmem(128, 512), vmem(128, 512), vmem(8, 128), vmem(128, 128), vmem(128, 128),
            vmem(4, 128, 128), vmem(4, 128, 128), vmem(4, 128, 128), vmem(4, 128, 128),
            vmem(4, 128, 128, dtype=BF16), vmem(4, 128, 128, dtype=BF16),
            vmem(4, 128, 128, dtype=BF16), vmem(4, 128, 128, dtype=BF16), vmem(2, 128, 128),
            vmem(4, 129, 128), vmem(4, 128, 128), vmem(4, 129, 128), vmem(4, 128, 128),
            vmem(16, 9, 128), vmem(16, 8, 128), vmem(16, 9, 128), vmem(16, 8, 128),
            vmem(16, 8, 128), vmem(16, 8, 128), vmem(128, 128), vmem(128, 128),
            vmem(4, 128, 128), vmem(4, 128, 128), vmem(4, 128, 128), vmem(4, 128, 128),
            vmem(2, 8, 16, 128), vmem(2, 8, 16, 128),
            dma(5), dma(2, 3), dma(2, 3), dma(2, 15), dma(2, 15), dma(2, 15), dma(2, 15), dma(2, 3), dma(2, 3),
            dma(2, 7), dma(2, 7), dma(2, 4),
        ],
        compiler_params=pltpu.CompilerParams(
            collective_id=0, has_side_effects=True, vmem_limit_bytes=32 * 1024 * 1024
        ),
    )(values, step_size, decay_rate, input_map, output_map, skip_gain, grad_output)
    piece = jax.ShapeDtypeStruct((16, 128), F32)
    return pl.pallas_call(
        hand_kernel,
        name="hand_over",
        out_shape=(full, full, piece, piece),
        in_specs=[anywhere] * 3,
        out_specs=(anywhere,) * 4,
        scratch_shapes=[pltpu.SemaphoreType.DMA((4,))],
    )(out, gv, maps)


def solution(mesh):
    placed = (
        P("ctx", "head"),
        P("head", "ctx"),
        P("head"),
        P("ctx", None),
        P("ctx", None),
        P("head"),
        P("ctx", "head"),
    )
    return jax.shard_map(
        shards,
        mesh=mesh,
        in_specs=placed,
        out_specs=(
            P("ctx", "head"),
            P("ctx", "head"),
            P(("ctx", "head"), None),
            P(("ctx", "head"), None),
        ),
        check_vma=False,
    )
```

```python
import functools

import jax
import jax.numpy as jnp
from jax import lax
from jax.experimental import pallas as pl
from jax.experimental.pallas import tpu as pltpu
from jax.sharding import PartitionSpec as P

MESH = pl.DeviceIdType.MESH
F32, BF16 = jnp.float32, jnp.bfloat16
NX, NZ, NH = 4, 16, 8
FAR_Z = (8, 7, 9, 6, 10, 5, 11, 4, 12, 3, 13, 2, 14, 1, 15)
FAR_X = (2, 1, 3)
FAR_H = (4, 5, 3, 6, 2, 7, 1)
NN = (((1,), (0,)), ((), ()))
NT = (((1,), (1,)), ((), ()))


def split(x):
    high = x.astype(BF16)
    return high, (x - high.astype(F32)).astype(BF16)


def dot3(a, b, dims=NN):
    (ah, al), (bh, bl) = a, b
    one = functools.partial(lax.dot_general, dimension_numbers=dims, preferred_element_type=F32)
    return one(ah, bh) + (one(al, bh) + one(ah, bl))


def core_kernel(
    v_hbm, step_hbm, rate_hbm, b_hbm, c_hbm, gain_hbm, g_hbm,
    out_hbm, gv_hbm, maps_hbm,
    v, g, step, bmap, cmap, rate, gain,
    out_acc, gv_acc, maps, from_w, end_w, gf_h, gf_l, xe_h, xe_l, local_maps,
    xs_f, xs_b, xr_f, xr_b, zs_f, zs_b, zr_f, zr_b, ys_f, ys_b, enter, leave, ws_f, ws_b, inc, fol, rs_s, rs_r,
    load_sem, x1_s, x1_r, z1_s, z1_r, z2_s, z2_r, x2_s, x2_r, rs_ss, rs_rs, out_sem,
):
    ctx, head = lax.axis_index("ctx"), lax.axis_index("head")
    mz, mx = ctx // NX, ctx % NX

    def at_x(d):
        return (mz * NX + lax.rem(mx + d, NX), head)

    def at_z(d):
        return (lax.rem(mz + d, NZ) * NX + mx, head)

    def at_h(d):
        return (ctx, lax.rem(head + d, NH))

    barrier = pltpu.get_barrier_semaphore()
    partners = [at_z(d) for d in FAR_Z] + [at_h(d) for d in FAR_H] + [at_x(d) for d in FAR_X]
    for partner in partners:
        pl.semaphore_signal(barrier, inc=1, device_id=partner, device_id_type=MESH)

    loads = [
        pltpu.make_async_copy(src, dst, load_sem.at[i])
        for i, (src, dst) in enumerate(
            ((step_hbm, step), (rate_hbm, rate), (b_hbm, bmap), (c_hbm, cmap), (v_hbm, v), (g_hbm, g), (gain_hbm, gain))
        )
    ]
    for load in loads:
        load.start()

    rows = lax.broadcasted_iota(jnp.int32, (128, 128), 0)
    lanes = lax.broadcasted_iota(jnp.int32, (128, 128), 1)
    first = lanes < 64
    lower = rows >= lanes
    upper = rows <= lanes

    loads[0].wait()
    loads[1].wait()
    steps = step[...]
    head_rows = lax.broadcasted_iota(jnp.int32, (NH, 128), 0)
    rates = jnp.zeros((NH, 128), F32)
    for h in range(NH):
        rates = jnp.where(head_rows == h, rate[h], rates)
    cum = lax.dot_general(
        steps * rates, jnp.where(upper, 1.0, 0.0).astype(F32), NN,
        precision=lax.Precision.HIGHEST, preferred_element_type=F32,
    )
    total = cum[:, 127:128]
    table = jnp.concatenate([steps, jnp.exp(cum), jnp.exp(total - cum), cum] + [jnp.zeros((96, 128), F32)], axis=0)
    table = table.T

    def column(kind, h):
        k = kind * NH + h
        return jnp.broadcast_to(table[:, k : k + 1], (128, 128))

    def pair(kind, q):
        return jnp.where(first, column(kind, 2 * q), column(kind, 2 * q + 1))

    loads[2].wait()
    loads[3].wait()
    b_all, c_all = bmap[...], cmap[...]
    b2, c2 = split(b_all), split(c_all)
    bt2, ct2 = split(b_all.T), split(c_all.T)
    loads[4].wait()
    loads[5].wait()
    loads[6].wait()

    scaled = []
    for q in range(NX):
        cols = slice(q * 128, (q + 1) * 128)
        step_w, start, end = pair(0, q), pair(1, q), pair(2, q)
        vq, gq = v[:, cols], g[:, cols]
        x = vq * step_w
        scaled.append(x)
        xe, gf = split(x * end), split(gq * start)
        xe_h[q], xe_l[q] = xe
        gf_h[q], gf_l[q] = gf
        from_w[q] = start
        end_w[q] = end * step_w
        xs_f[q, 0:128, :] = dot3(bt2, xe)
        xs_f[q, 128:129, :] = start[127:128, :]
        xs_b[q] = dot3(ct2, gf)

    pl.semaphore_wait(barrier, len(partners))

    def send(src, dst, send_sem, recv_sem, partner):
        copy = pltpu.make_async_remote_copy(
            src_ref=src, dst_ref=dst, send_sem=send_sem, recv_sem=recv_sem, device_id=partner, device_id_type=MESH
        )
        copy.start()
        return copy

    sent = []

    x1 = []
    for i, (source, target) in enumerate(((xs_f, xr_f), (xs_b, xr_b))):
        x1.append([
            send(source.at[lax.rem(mx + d, NX)], target.at[mx], x1_s.at[i, d - 1], x1_r.at[i, d - 1], at_x(d))
            for d in FAR_X
        ])
        target[mx] = source[mx]
    sent += x1[0] + x1[1]

    z1 = []
    for copy in x1[0]:
        copy.wait_recv()
    decays = [xr_f[k, 128:129, :] for k in range(NX)]
    acc = xr_f[0, 0:128, :]
    for k in range(1, NX):
        acc = acc * decays[k] + xr_f[k, 0:128, :]
    plane = decays[0] * decays[1] * decays[2] * decays[3]
    for j in range(NZ):
        zs_f[j, 0:8, :] = acc[8 * j : 8 * j + 8, :]
        zs_f[j, 8:9, :] = plane
    z1.append([
        send(zs_f.at[lax.rem(mz + d, NZ)], zr_f.at[mz], z1_s.at[0, d - 1], z1_r.at[0, d - 1], at_z(d)) for d in FAR_Z
    ])
    zr_f[mz] = zs_f[mz]
    for copy in x1[1]:
        copy.wait_recv()
    acc = xr_b[NX - 1]
    for k in range(NX - 2, -1, -1):
        acc = acc * decays[k] + xr_b[k]
    for j in range(NZ):
        zs_b[j] = acc[8 * j : 8 * j + 8, :]
    z1.append([
        send(zs_b.at[lax.rem(mz + d, NZ)], zr_b.at[mz], z1_s.at[1, d - 1], z1_r.at[1, d - 1], at_z(d)) for d in FAR_Z
    ])
    zr_b[mz] = zs_b[mz]
    sent += z1[0] + z1[1]

    scores, scores_t = dot3(c2, b2, NT), dot3(b2, c2, NT)
    inner = jnp.zeros((128, 128), F32)
    for q in range(NX):
        cols = slice(q * 128, (q + 1) * 128)
        x, gq = scaled[q], g[:, cols]
        x2, g2 = split(x), split(gq)
        outs, grads = [], []
        for k in range(2):
            h = 2 * q + k
            mine = first if k == 0 else jnp.logical_not(first)
            gap = column(3, h) - cum[h : h + 1, :]
            decay = jnp.exp(jnp.where(lower, gap, -gap))
            below = jnp.where(lower, decay, 0.0)
            above = jnp.where(upper, decay, 0.0)
            part = split(jnp.where(mine, gq, 0.0))
            inner = inner + dot3(part, x2, NT) * below
            outs.append(dot3(split(scores * below), x2))
            grads.append(dot3(split(scores_t * above), g2))
        skip = jnp.where(first[0:1], gain[2 * q], gain[2 * q + 1])
        step_w = pair(0, q)
        out_acc[q] = jnp.where(first, outs[0], outs[1]) + skip * v[:, cols]
        gv_acc[q] = step_w * jnp.where(first, grads[0], grads[1]) + skip * gq
    local_maps[0] = dot3(split(inner), b2)
    local_maps[1] = dot3(split(inner.T), c2)

    z2 = []
    mine_rows = pl.ds(pl.multiple_of(mz * 8, 8), 8)
    for copy in z1[0]:
        copy.wait_recv()
    carry = jnp.zeros((8, 128), F32)
    for j in range(NZ):
        ys_f[j] = carry
        carry = carry * zr_f[j, 8:9, :] + zr_f[j, 0:8, :]
    z2.append([
        send(ys_f.at[lax.rem(mz + d, NZ)], enter.at[mine_rows], z2_s.at[0, d - 1], z2_r.at[0, d - 1], at_z(d))
        for d in FAR_Z
    ])
    enter[mine_rows, :] = ys_f[mz]
    for copy in z1[1]:
        copy.wait_recv()
    carry = jnp.zeros((8, 128), F32)
    for j in range(NZ - 1, -1, -1):
        ys_b[j] = carry
        carry = carry * zr_f[j, 8:9, :] + zr_b[j]
    z2.append([
        send(ys_b.at[lax.rem(mz + d, NZ)], leave.at[mine_rows], z2_s.at[1, d - 1], z2_r.at[1, d - 1], at_z(d))
        for d in FAR_Z
    ])
    leave[mine_rows, :] = ys_b[mz]
    sent += z2[0] + z2[1]

    x2 = []
    for copy in z2[0]:
        copy.wait_recv()
    carry = enter[...]
    for k in range(NX):
        ws_f[k] = carry
        if k < NX - 1:
            carry = carry * decays[k] + xr_f[k, 0:128, :]
    x2.append([
        send(ws_f.at[lax.rem(mx + d, NX)], inc.at[mx], x2_s.at[0, d - 1], x2_r.at[0, d - 1], at_x(d)) for d in FAR_X
    ])
    inc[mx] = ws_f[mx]
    for copy in z2[1]:
        copy.wait_recv()
    carry = leave[...]
    for k in range(NX - 1, -1, -1):
        ws_b[k] = carry
        if k > 0:
            carry = carry * decays[k] + xr_b[k]
    x2.append([
        send(ws_b.at[lax.rem(mx + d, NX)], fol.at[mx], x2_s.at[1, d - 1], x2_r.at[1, d - 1], at_x(d)) for d in FAR_X
    ])
    fol[mx] = ws_b[mx]
    sent += x2[0] + x2[1]

    rs, stores = [], []
    plans = (
        (inc, c2, gf_h, gf_l, from_w, out_acc, out_hbm),
        (fol, b2, xe_h, xe_l, end_w, gv_acc, gv_hbm),
    )
    for i, (carried, map2, w_h, w_l, weight, acc_ref, hbm) in enumerate(plans):
        grad = local_maps[i]
        states = []
        for copy, d in zip([None] + x2[i], (0,) + FAR_X):
            if copy is not None:
                copy.wait_recv()
            q = lax.rem(mx + NX - d, NX)
            state2 = split(carried[q])
            states.append((q, state2))
            grad = grad + dot3((w_h[q], w_l[q]), state2, NT)
        for k in range(NH):
            rs_s[i, k] = grad[16 * k : 16 * k + 16, :]
        rs.append([
            send(rs_s.at[i, lax.rem(head + d, NH)], rs_r.at[i, head], rs_ss.at[i, d - 1], rs_rs.at[i, d - 1], at_h(d))
            for d in FAR_H
        ])
        rs_r[i, head] = rs_s[i, head]
        for n, (q, state2) in enumerate(states):
            acc_ref[q] = acc_ref[q] + weight[q] * dot3(map2, state2)
            cols = pl.ds(pl.multiple_of(q * 128, 128), 128)
            store = pltpu.make_async_copy(acc_ref.at[q], hbm.at[:, cols], out_sem.at[i, n])
            store.start()
            stores.append(store)
    sent += rs[0] + rs[1]
    for i in range(2):
        for copy in rs[i]:
            copy.wait_recv()
        whole = rs_r[i, 0]
        for k in range(1, NH):
            whole = whole + rs_r[i, k]
        maps[i] = whole
        store = pltpu.make_async_copy(maps.at[i], maps_hbm.at[i], out_sem.at[i, NX])
        store.start()
        stores.append(store)
    for copy in stores:
        copy.wait()
    for copy in sent:
        copy.wait_send()


def hand_kernel(out_in, gv_in, maps_in, out, gv, gi, go, wide, small, sem):
    pairs = (
        (out_in, wide.at[0], out), (gv_in, wide.at[1], gv), (maps_in.at[1], small.at[1], gi), (maps_in.at[0], small.at[0], go)
    )
    loads = [pltpu.make_async_copy(src, via, sem.at[0, i]) for i, (src, via, _) in enumerate(pairs)]
    stores = [pltpu.make_async_copy(via, dst, sem.at[1, i]) for i, (_, via, dst) in enumerate(pairs)]
    for copy in loads:
        copy.start()
    for load, store in zip(loads, stores):
        load.wait()
        store.start()
    for copy in stores:
        copy.wait()


def shards(values, step_size, decay_rate, input_map, output_map, skip_gain, grad_output):
    far = pl.BlockSpec(memory_space=pltpu.HBM)
    vmem = lambda *shape, dtype=F32: pltpu.VMEM(shape, dtype)
    dma = lambda *shape: pltpu.SemaphoreType.DMA(shape)
    full = jax.ShapeDtypeStruct(values.shape, F32)
    out, gv, maps = pl.pallas_call(
        core_kernel,
        name="scan_core",
        out_shape=(full, full, jax.ShapeDtypeStruct((2, 16, 128), F32)),
        in_specs=[far] * 7,
        out_specs=(far,) * 3,
        scratch_shapes=[
            vmem(128, 512), vmem(128, 512), vmem(8, 128), vmem(128, 128), vmem(128, 128),
            pltpu.SMEM((8,), F32), pltpu.SMEM((8,), F32),
            vmem(4, 128, 128), vmem(4, 128, 128), vmem(2, 16, 128), vmem(4, 128, 128), vmem(4, 128, 128),
            vmem(4, 128, 128, dtype=BF16), vmem(4, 128, 128, dtype=BF16),
            vmem(4, 128, 128, dtype=BF16), vmem(4, 128, 128, dtype=BF16), vmem(2, 128, 128),
            vmem(4, 129, 128), vmem(4, 128, 128), vmem(4, 129, 128), vmem(4, 128, 128),
            vmem(16, 9, 128), vmem(16, 8, 128), vmem(16, 9, 128), vmem(16, 8, 128),
            vmem(16, 8, 128), vmem(16, 8, 128), vmem(128, 128), vmem(128, 128),
            vmem(4, 128, 128), vmem(4, 128, 128), vmem(4, 128, 128), vmem(4, 128, 128),
            vmem(2, 8, 16, 128), vmem(2, 8, 16, 128),
            dma(7), dma(2, 3), dma(2, 3), dma(2, 15), dma(2, 15), dma(2, 15), dma(2, 15), dma(2, 3), dma(2, 3),
            dma(2, 7), dma(2, 7), dma(2, 5),
        ],
        compiler_params=pltpu.CompilerParams(
            collective_id=0, has_side_effects=True, vmem_limit_bytes=60 * 1024 * 1024
        ),
    )(values, step_size, decay_rate, input_map, output_map, skip_gain, grad_output)
    piece = jax.ShapeDtypeStruct((16, 128), F32)
    return pl.pallas_call(
        hand_kernel,
        name="hand_over",
        out_shape=(full, full, piece, piece),
        in_specs=[far] * 3,
        out_specs=(far,) * 4,
        scratch_shapes=[vmem(2, 128, 512), vmem(2, 16, 128), dma(2, 4)],
    )(out, gv, maps)


def solution(mesh):
    placed = (
        P("ctx", "head"),
        P("head", "ctx"),
        P("head"),
        P("ctx", None),
        P("ctx", None),
        P("head"),
        P("ctx", "head"),
    )
    return jax.shard_map(
        shards,
        mesh=mesh,
        in_specs=placed,
        out_specs=(
            P("ctx", "head"),
            P("ctx", "head"),
            P(("ctx", "head"), None),
            P(("ctx", "head"), None),
        ),
        check_vma=False,
    )
```

```python
import functools

import jax
import jax.numpy as jnp
from jax import lax
from jax.experimental import pallas as pl
from jax.experimental.pallas import tpu as pltpu
from jax.sharding import PartitionSpec as P

MESH = pl.DeviceIdType.MESH
F32, BF16 = jnp.float32, jnp.bfloat16
NX, NZ, NH = 4, 16, 8
FAR_Z = (8, 7, 9, 6, 10, 5, 11, 4, 12, 3, 13, 2, 14, 1, 15)
NEAR_Z = (4, 12, 3, 13, 2, 14, 1, 15)
FAR_X = (2, 1, 3)
FAR_H = (4, 5, 3, 6, 2, 7, 1)
NN = (((1,), (0,)), ((), ()))
NT = (((1,), (1,)), ((), ()))


def split(x):
    high = x.astype(BF16)
    return high, (x - high.astype(F32)).astype(BF16)


def dot3(a, b, dims=NN):
    (ah, al), (bh, bl) = a, b
    one = functools.partial(lax.dot_general, dimension_numbers=dims, preferred_element_type=F32)
    return one(ah, bh) + (one(al, bh) + one(ah, bl))


def core_kernel(
    v_hbm, step_hbm, rate_hbm, b_hbm, c_hbm, gain_hbm, g_hbm,
    out_hbm, gv_hbm, maps_hbm,
    v, g, step, bmap, cmap, rate, gain,
    out_acc, gv_acc, maps, from_w, end_w, gf_h, gf_l, xe_h, xe_l, local_maps,
    xs_f, xs_b, xr_f, xr_b, zs_f, zs_b, zr_f, zr_b, ys_f, ys_b, enter, leave, ws_f, ws_b, inc, fol, rs_s, rs_r,
    reach, load_sem, x1_s, x1_r, z1_s, z1_r, z2_s, z2_r, x2_s, x2_r, rs_ss, rs_rs, out_sem,
):
    ctx, head = lax.axis_index("ctx"), lax.axis_index("head")
    mz, mx = ctx // NX, ctx % NX

    def at_x(d):
        return (mz * NX + lax.rem(mx + d, NX), head)

    def at_z(d):
        return (lax.rem(mz + d, NZ) * NX + mx, head)

    def at_h(d):
        return (ctx, lax.rem(head + d, NH))

    barrier = pltpu.get_barrier_semaphore()
    partners = [at_z(d) for d in NEAR_Z] + [at_h(d) for d in FAR_H] + [at_x(d) for d in FAR_X]
    for partner in partners:
        pl.semaphore_signal(barrier, inc=1, device_id=partner, device_id_type=MESH)

    loads = [
        pltpu.make_async_copy(src, dst, load_sem.at[i])
        for i, (src, dst) in enumerate(
            ((step_hbm, step), (rate_hbm, rate), (b_hbm, bmap), (c_hbm, cmap), (v_hbm, v), (g_hbm, g), (gain_hbm, gain))
        )
    ]
    for load in loads:
        load.start()

    rows = lax.broadcasted_iota(jnp.int32, (128, 128), 0)
    lanes = lax.broadcasted_iota(jnp.int32, (128, 128), 1)
    first = lanes < 64
    lower = rows >= lanes
    upper = rows <= lanes

    loads[0].wait()
    loads[1].wait()
    steps = step[...]
    head_rows = lax.broadcasted_iota(jnp.int32, (NH, 128), 0)
    rates = jnp.zeros((NH, 128), F32)
    for h in range(NH):
        rates = jnp.where(head_rows == h, rate[h], rates)
    cum = lax.dot_general(
        steps * rates, jnp.where(upper, 1.0, 0.0).astype(F32), NN,
        precision=lax.Precision.HIGHEST, preferred_element_type=F32,
    )
    total = cum[:, 127:128]
    table = jnp.concatenate([steps, jnp.exp(cum), jnp.exp(total - cum), cum] + [jnp.zeros((96, 128), F32)], axis=0)
    table = table.T

    def column(kind, h):
        k = kind * NH + h
        return jnp.broadcast_to(table[:, k : k + 1], (128, 128))

    def pair(kind, q):
        return jnp.where(first, column(kind, 2 * q), column(kind, 2 * q + 1))

    loads[2].wait()
    loads[3].wait()
    b_all, c_all = bmap[...], cmap[...]
    b2, c2 = split(b_all), split(c_all)
    bt2, ct2 = split(b_all.T), split(c_all.T)
    loads[4].wait()
    loads[5].wait()
    loads[6].wait()

    scaled = []
    for q in range(NX):
        cols = slice(q * 128, (q + 1) * 128)
        step_w, start, end = pair(0, q), pair(1, q), pair(2, q)
        vq, gq = v[:, cols], g[:, cols]
        x = vq * step_w
        scaled.append(x)
        xe, gf = split(x * end), split(gq * start)
        xe_h[q], xe_l[q] = xe
        gf_h[q], gf_l[q] = gf
        from_w[q] = start
        end_w[q] = end * step_w
        xs_f[q, 0:128, :] = dot3(bt2, xe)
        xs_f[q, 128:129, :] = start[127:128, :]
        xs_b[q] = dot3(ct2, gf)

    pl.semaphore_wait(barrier, len(partners))
    for d in (4, 12):
        pl.semaphore_signal(reach, inc=1, device_id=at_z(d), device_id_type=MESH)

    def send(src, dst, send_sem, recv_sem, partner):
        copy = pltpu.make_async_remote_copy(
            src_ref=src, dst_ref=dst, send_sem=send_sem, recv_sem=recv_sem, device_id=partner, device_id_type=MESH
        )
        copy.start()
        return copy

    sent = []

    x1 = []
    for i, (source, target) in enumerate(((xs_f, xr_f), (xs_b, xr_b))):
        x1.append([
            send(source.at[lax.rem(mx + d, NX)], target.at[mx], x1_s.at[i, d - 1], x1_r.at[i, d - 1], at_x(d))
            for d in FAR_X
        ])
        target[mx] = source[mx]
    sent += x1[0] + x1[1]

    z1 = []
    for copy in x1[0]:
        copy.wait_recv()
    decays = [xr_f[k, 128:129, :] for k in range(NX)]
    acc = xr_f[0, 0:128, :]
    for k in range(1, NX):
        acc = acc * decays[k] + xr_f[k, 0:128, :]
    plane = decays[0] * decays[1] * decays[2] * decays[3]
    for j in range(NZ):
        zs_f[j, 0:8, :] = acc[8 * j : 8 * j + 8, :]
        zs_f[j, 8:9, :] = plane
    pl.semaphore_wait(reach, 2)
    z1.append([
        send(zs_f.at[lax.rem(mz + d, NZ)], zr_f.at[mz], z1_s.at[0, d - 1], z1_r.at[0, d - 1], at_z(d)) for d in FAR_Z
    ])
    zr_f[mz] = zs_f[mz]
    for copy in x1[1]:
        copy.wait_recv()
    acc = xr_b[NX - 1]
    for k in range(NX - 2, -1, -1):
        acc = acc * decays[k] + xr_b[k]
    for j in range(NZ):
        zs_b[j] = acc[8 * j : 8 * j + 8, :]
    z1.append([
        send(zs_b.at[lax.rem(mz + d, NZ)], zr_b.at[mz], z1_s.at[1, d - 1], z1_r.at[1, d - 1], at_z(d)) for d in FAR_Z
    ])
    zr_b[mz] = zs_b[mz]
    sent += z1[0] + z1[1]

    scores, scores_t = dot3(c2, b2, NT), dot3(b2, c2, NT)
    inner = jnp.zeros((128, 128), F32)
    for q in range(NX):
        cols = slice(q * 128, (q + 1) * 128)
        x, gq = scaled[q], g[:, cols]
        x2, g2 = split(x), split(gq)
        outs, grads = [], []
        for k in range(2):
            h = 2 * q + k
            mine = first if k == 0 else jnp.logical_not(first)
            gap = column(3, h) - cum[h : h + 1, :]
            decay = jnp.exp(jnp.where(lower, gap, -gap))
            below = jnp.where(lower, decay, 0.0)
            above = jnp.where(upper, decay, 0.0)
            part = split(jnp.where(mine, gq, 0.0))
            inner = inner + dot3(part, x2, NT) * below
            outs.append(dot3(split(scores * below), x2))
            grads.append(dot3(split(scores_t * above), g2))
        skip = jnp.where(first[0:1], gain[2 * q], gain[2 * q + 1])
        step_w = pair(0, q)
        out_acc[q] = jnp.where(first, outs[0], outs[1]) + skip * v[:, cols]
        gv_acc[q] = step_w * jnp.where(first, grads[0], grads[1]) + skip * gq
    local_maps[0] = dot3(split(inner), b2)
    local_maps[1] = dot3(split(inner.T), c2)

    z2 = []
    mine_rows = pl.ds(pl.multiple_of(mz * 8, 8), 8)
    for copy in z1[0]:
        copy.wait_recv()
    carry = jnp.zeros((8, 128), F32)
    for j in range(NZ):
        ys_f[j] = carry
        carry = carry * zr_f[j, 8:9, :] + zr_f[j, 0:8, :]
    z2.append([
        send(ys_f.at[lax.rem(mz + d, NZ)], enter.at[mine_rows], z2_s.at[0, d - 1], z2_r.at[0, d - 1], at_z(d))
        for d in FAR_Z
    ])
    enter[mine_rows, :] = ys_f[mz]
    for copy in z1[1]:
        copy.wait_recv()
    carry = jnp.zeros((8, 128), F32)
    for j in range(NZ - 1, -1, -1):
        ys_b[j] = carry
        carry = carry * zr_f[j, 8:9, :] + zr_b[j]
    z2.append([
        send(ys_b.at[lax.rem(mz + d, NZ)], leave.at[mine_rows], z2_s.at[1, d - 1], z2_r.at[1, d - 1], at_z(d))
        for d in FAR_Z
    ])
    leave[mine_rows, :] = ys_b[mz]
    sent += z2[0] + z2[1]

    x2 = []
    for copy in z2[0]:
        copy.wait_recv()
    carry = enter[...]
    for k in range(NX):
        ws_f[k] = carry
        if k < NX - 1:
            carry = carry * decays[k] + xr_f[k, 0:128, :]
    x2.append([
        send(ws_f.at[lax.rem(mx + d, NX)], inc.at[mx], x2_s.at[0, d - 1], x2_r.at[0, d - 1], at_x(d)) for d in FAR_X
    ])
    inc[mx] = ws_f[mx]
    for copy in z2[1]:
        copy.wait_recv()
    carry = leave[...]
    for k in range(NX - 1, -1, -1):
        ws_b[k] = carry
        if k > 0:
            carry = carry * decays[k] + xr_b[k]
    x2.append([
        send(ws_b.at[lax.rem(mx + d, NX)], fol.at[mx], x2_s.at[1, d - 1], x2_r.at[1, d - 1], at_x(d)) for d in FAR_X
    ])
    fol[mx] = ws_b[mx]
    sent += x2[0] + x2[1]

    rs, stores = [], []
    plans = (
        (inc, c2, gf_h, gf_l, from_w, out_acc, out_hbm),
        (fol, b2, xe_h, xe_l, end_w, gv_acc, gv_hbm),
    )
    for i, (carried, map2, w_h, w_l, weight, acc_ref, hbm) in enumerate(plans):
        grad = local_maps[i]
        states = []
        for copy, d in zip([None] + x2[i], (0,) + FAR_X):
            if copy is not None:
                copy.wait_recv()
            q = lax.rem(mx + NX - d, NX)
            state2 = split(carried[q])
            states.append((q, state2))
            grad = grad + dot3((w_h[q], w_l[q]), state2, NT)
        for k in range(NH):
            rs_s[i, k] = grad[16 * k : 16 * k + 16, :]
        rs.append([
            send(rs_s.at[i, lax.rem(head + d, NH)], rs_r.at[i, head], rs_ss.at[i, d - 1], rs_rs.at[i, d - 1], at_h(d))
            for d in FAR_H
        ])
        rs_r[i, head] = rs_s[i, head]
        for n, (q, state2) in enumerate(states):
            acc_ref[q] = acc_ref[q] + weight[q] * dot3(map2, state2)
            cols = pl.ds(pl.multiple_of(q * 128, 128), 128)
            store = pltpu.make_async_copy(acc_ref.at[q], hbm.at[:, cols], out_sem.at[i, n])
            store.start()
            stores.append(store)
    sent += rs[0] + rs[1]
    for i in range(2):
        for copy in rs[i]:
            copy.wait_recv()
        whole = rs_r[i, 0]
        for k in range(1, NH):
            whole = whole + rs_r[i, k]
        maps[i] = whole
        store = pltpu.make_async_copy(maps.at[i], maps_hbm.at[i], out_sem.at[i, NX])
        store.start()
        stores.append(store)
    for copy in stores:
        copy.wait()
    for copy in sent:
        copy.wait_send()


def hand_kernel(out_in, gv_in, maps_in, out, gv, gi, go, wide, small, sem):
    pairs = (
        (out_in, wide.at[0], out), (gv_in, wide.at[1], gv), (maps_in.at[1], small.at[1], gi), (maps_in.at[0], small.at[0], go)
    )
    loads = [pltpu.make_async_copy(src, via, sem.at[0, i]) for i, (src, via, _) in enumerate(pairs)]
    stores = [pltpu.make_async_copy(via, dst, sem.at[1, i]) for i, (_, via, dst) in enumerate(pairs)]
    for copy in loads:
        copy.start()
    for load, store in zip(loads, stores):
        load.wait()
        store.start()
    for copy in stores:
        copy.wait()


def shards(values, step_size, decay_rate, input_map, output_map, skip_gain, grad_output):
    far = pl.BlockSpec(memory_space=pltpu.HBM)
    vmem = lambda *shape, dtype=F32: pltpu.VMEM(shape, dtype)
    dma = lambda *shape: pltpu.SemaphoreType.DMA(shape)
    full = jax.ShapeDtypeStruct(values.shape, F32)
    out, gv, maps = pl.pallas_call(
        core_kernel,
        name="scan_core",
        out_shape=(full, full, jax.ShapeDtypeStruct((2, 16, 128), F32)),
        in_specs=[far] * 7,
        out_specs=(far,) * 3,
        scratch_shapes=[
            vmem(128, 512), vmem(128, 512), vmem(8, 128), vmem(128, 128), vmem(128, 128),
            pltpu.SMEM((8,), F32), pltpu.SMEM((8,), F32),
            vmem(4, 128, 128), vmem(4, 128, 128), vmem(2, 16, 128), vmem(4, 128, 128), vmem(4, 128, 128),
            vmem(4, 128, 128, dtype=BF16), vmem(4, 128, 128, dtype=BF16),
            vmem(4, 128, 128, dtype=BF16), vmem(4, 128, 128, dtype=BF16), vmem(2, 128, 128),
            vmem(4, 129, 128), vmem(4, 128, 128), vmem(4, 129, 128), vmem(4, 128, 128),
            vmem(16, 9, 128), vmem(16, 8, 128), vmem(16, 9, 128), vmem(16, 8, 128),
            vmem(16, 8, 128), vmem(16, 8, 128), vmem(128, 128), vmem(128, 128),
            vmem(4, 128, 128), vmem(4, 128, 128), vmem(4, 128, 128), vmem(4, 128, 128),
            vmem(2, 8, 16, 128), vmem(2, 8, 16, 128),
            pltpu.SemaphoreType.REGULAR, dma(7), dma(2, 3), dma(2, 3), dma(2, 15), dma(2, 15), dma(2, 15), dma(2, 15), dma(2, 3), dma(2, 3),
            dma(2, 7), dma(2, 7), dma(2, 5),
        ],
        compiler_params=pltpu.CompilerParams(
            collective_id=0, has_side_effects=True, vmem_limit_bytes=60 * 1024 * 1024
        ),
    )(values, step_size, decay_rate, input_map, output_map, skip_gain, grad_output)
    piece = jax.ShapeDtypeStruct((16, 128), F32)
    return pl.pallas_call(
        hand_kernel,
        name="hand_over",
        out_shape=(full, full, piece, piece),
        in_specs=[far] * 3,
        out_specs=(far,) * 4,
        scratch_shapes=[vmem(2, 128, 512), vmem(2, 16, 128), dma(2, 4)],
    )(out, gv, maps)


def solution(mesh):
    placed = (
        P("ctx", "head"),
        P("head", "ctx"),
        P("head"),
        P("ctx", None),
        P("ctx", None),
        P("head"),
        P("ctx", "head"),
    )
    return jax.shard_map(
        shards,
        mesh=mesh,
        in_specs=placed,
        out_specs=(
            P("ctx", "head"),
            P("ctx", "head"),
            P(("ctx", "head"), None),
            P(("ctx", "head"), None),
        ),
        check_vma=False,
    )
```

```python
import functools

import jax
import jax.numpy as jnp
from jax import lax
from jax.experimental import pallas as pl
from jax.experimental.pallas import tpu as pltpu
from jax.sharding import PartitionSpec as P

MESH = pl.DeviceIdType.MESH
F32, BF16 = jnp.float32, jnp.bfloat16
NX, NZ, NH = 4, 16, 8
EARLY = 4
FAR_Z = (8, 7, 9, 6, 10, 5, 11, 4, 12, 3, 13, 2, 14, 1, 15)
NEAR_Z = (4, 12, 3, 13, 2, 14, 1, 15)
FAR_X = (2, 1, 3)
FAR_H = (4, 5, 3, 6, 2, 7, 1)
NN = (((1,), (0,)), ((), ()))
NT = (((1,), (1,)), ((), ()))


def split(x):
    high = x.astype(BF16)
    return high, (x - high.astype(F32)).astype(BF16)


def dot3(a, b, dims=NN):
    (ah, al), (bh, bl) = a, b
    one = functools.partial(lax.dot_general, dimension_numbers=dims, preferred_element_type=F32)
    return one(ah, bh) + (one(al, bh) + one(ah, bl))


def core_kernel(
    v_hbm, step_hbm, rate_hbm, b_hbm, c_hbm, gain_hbm, g_hbm,
    out_hbm, gv_hbm, maps_hbm,
    v, g, step, bmap, cmap, rate, gain,
    out_acc, gv_acc, maps, from_w, end_w, gf_h, gf_l, xe_h, xe_l, local_maps,
    xs_f, xs_b, xr_f, xr_b, zs_f, zs_b, zr_f, zr_b, ys_f, ys_b, enter, leave, handed, total_f, ws_f, ws_b, inc, fol, rs_s, rs_r,
    reach, hand_s, hand_r, load_sem, x1_s, x1_r, z1_s, z1_r, z2_s, z2_r, x2_s, x2_r, rs_ss, rs_rs, out_sem,
):
    ctx, head = lax.axis_index("ctx"), lax.axis_index("head")
    mz, mx = ctx // NX, ctx % NX

    def at_x(d):
        return (mz * NX + lax.rem(mx + d, NX), head)

    def at_z(d):
        return (lax.rem(mz + d, NZ) * NX + mx, head)

    def at_h(d):
        return (ctx, lax.rem(head + d, NH))

    barrier = pltpu.get_barrier_semaphore()
    partners = [at_z(d) for d in NEAR_Z] + [at_h(d) for d in FAR_H] + [at_x(d) for d in FAR_X]
    for partner in partners:
        pl.semaphore_signal(barrier, inc=1, device_id=partner, device_id_type=MESH)

    loads = [
        pltpu.make_async_copy(src, dst, load_sem.at[i])
        for i, (src, dst) in enumerate(
            ((step_hbm, step), (rate_hbm, rate), (b_hbm, bmap), (c_hbm, cmap), (v_hbm, v), (g_hbm, g), (gain_hbm, gain))
        )
    ]
    for load in loads:
        load.start()

    rows = lax.broadcasted_iota(jnp.int32, (128, 128), 0)
    lanes = lax.broadcasted_iota(jnp.int32, (128, 128), 1)
    first = lanes < 64
    lower = rows >= lanes
    upper = rows <= lanes

    loads[0].wait()
    loads[1].wait()
    steps = step[...]
    head_rows = lax.broadcasted_iota(jnp.int32, (NH, 128), 0)
    rates = jnp.zeros((NH, 128), F32)
    for h in range(NH):
        rates = jnp.where(head_rows == h, rate[h], rates)
    cum = lax.dot_general(
        steps * rates, jnp.where(upper, 1.0, 0.0).astype(F32), NN,
        precision=lax.Precision.HIGHEST, preferred_element_type=F32,
    )
    total = cum[:, 127:128]
    table = jnp.concatenate([steps, jnp.exp(cum), jnp.exp(total - cum), cum] + [jnp.zeros((96, 128), F32)], axis=0)
    table = table.T

    def column(kind, h):
        k = kind * NH + h
        return jnp.broadcast_to(table[:, k : k + 1], (128, 128))

    def pair(kind, q):
        return jnp.where(first, column(kind, 2 * q), column(kind, 2 * q + 1))

    loads[2].wait()
    loads[3].wait()
    b_all, c_all = bmap[...], cmap[...]
    b2, c2 = split(b_all), split(c_all)
    bt2, ct2 = split(b_all.T), split(c_all.T)
    loads[4].wait()
    loads[5].wait()
    loads[6].wait()

    scaled = []
    for q in range(NX):
        cols = slice(q * 128, (q + 1) * 128)
        step_w, start, end = pair(0, q), pair(1, q), pair(2, q)
        vq, gq = v[:, cols], g[:, cols]
        x = vq * step_w
        scaled.append(x)
        xe, gf = split(x * end), split(gq * start)
        xe_h[q], xe_l[q] = xe
        gf_h[q], gf_l[q] = gf
        from_w[q] = start
        end_w[q] = end * step_w
        xs_b[q, 0:128, :] = dot3(ct2, gf)
        xs_b[q, 128:129, :] = start[127:128, :]
        xs_f[q, 0:128, :] = dot3(bt2, xe)
        xs_f[q, 128:129, :] = start[127:128, :]

    pl.semaphore_wait(barrier, len(partners))
    for d in (4, 12):
        pl.semaphore_signal(reach, inc=1, device_id=at_z(d), device_id_type=MESH)

    def remote(src, dst, send_sem, recv_sem, partner):
        return pltpu.make_async_remote_copy(
            src_ref=src, dst_ref=dst, send_sem=send_sem, recv_sem=recv_sem, device_id=partner, device_id_type=MESH
        )

    mine_rows = pl.ds(pl.multiple_of(mz * 8, 8), 8)
    xs, xr, zs, zr, ys, carried_in = (xs_b, xs_f), (xr_b, xr_f), (zs_b, zs_f), (zr_b, zr_f), (ys_b, ys_f), (leave, enter)
    ws, states_in = (ws_b, ws_f), (fol, inc)
    x1 = [[
        remote(xs[i].at[lax.rem(mx + d, NX)], xr[i].at[mx], x1_s.at[i, d - 1], x1_r.at[i, d - 1], at_x(d)) for d in FAR_X
    ] for i in range(2)]
    z1 = [[
        remote(zs[i].at[lax.rem(mz + d, NZ)], zr[i].at[mz], z1_s.at[i, d - 1], z1_r.at[i, d - 1], at_z(d)) for d in FAR_Z
    ] for i in range(2)]
    z2 = [[
        remote(
            ys[i].at[lax.rem(mz + d, NZ)], carried_in[i].at[mine_rows], z2_s.at[i, d - 1], z2_r.at[i, d - 1], at_z(d)
        ) for d in FAR_Z
    ] for i in range(2)]
    x2 = [[
        remote(ws[i].at[lax.rem(mx + d, NX)], states_in[i].at[mx], x2_s.at[i, d - 1], x2_r.at[i, d - 1], at_x(d))
        for d in FAR_X
    ] for i in range(2)]
    rs = [[
        remote(rs_s.at[i, lax.rem(head + d, NH)], rs_r.at[i, head], rs_ss.at[i, d - 1], rs_rs.at[i, d - 1], at_h(d))
        for d in FAR_H
    ] for i in range(2)]

    def x1_send(i):
        for copy in x1[i]:
            copy.start()

    @pl.when(mz == 0)
    def _():
        x1_send(1)
        x1_send(0)

    @pl.when(mz != 0)
    def _():
        x1_send(0)
        x1_send(1)

    for i in range(2):
        xr[i][mx] = xs[i][mx]

    def decay(i, k):
        return xr[i][k, 128:129, :]

    def backward_z1():
        for copy in x1[0]:
            copy.wait_recv()
        acc = xr_b[NX - 1, 0:128, :]
        for k in range(NX - 2, -1, -1):
            acc = acc * decay(0, k) + xr_b[k, 0:128, :]
        plane = decay(0, 0) * decay(0, 1) * decay(0, 2) * decay(0, 3)
        for j in range(NZ):
            zs_b[j, 0:8, :] = acc[8 * j : 8 * j + 8, :]
            zs_b[j, 8:9, :] = plane
        pl.semaphore_wait(reach, 2)
        for copy in z1[0]:
            copy.start()
        zr_b[mz] = zs_b[mz]

    def forward_total():
        for copy in x1[1]:
            copy.wait_recv()
        acc = xr_f[0, 0:128, :]
        for k in range(1, NX):
            acc = acc * decay(1, k) + xr_f[k, 0:128, :]
        total_f[...] = acc
        for j in range(NZ):
            zs_f[j] = acc[8 * j : 8 * j + 8, :]

    def forward_z1():
        for copy in z1[1]:
            pl.when(mz != NZ - 1)(copy.start)
        zr_f[mz] = zs_f[mz]

    early = mz < EARLY
    hand_on = remote(handed, enter, hand_s, hand_r, at_z(1))

    def hand_over_state():
        plane = decay(1, 0) * decay(1, 1) * decay(1, 2) * decay(1, 3)
        handed[...] = enter[...] * plane + total_f[...]
        hand_on.start()

    def forward_x2():
        carry = enter[...]
        for k in range(NX):
            ws_f[k] = carry
            if k < NX - 1:
                carry = carry * decay(1, k) + xr_f[k, 0:128, :]
        for copy in x2[1]:
            copy.start()
        inc[mx] = ws_f[mx]

    def backward_x2(carry):
        for k in range(NX - 1, -1, -1):
            ws_b[k] = carry
            if k > 0:
                carry = carry * decay(0, k) + xr_b[k, 0:128, :]
        for copy in x2[0]:
            copy.start()
        fol[mx] = ws_b[mx]

    def last(i):
        carried, map2, w_h, w_l, weight, acc_ref, hbm = (
            (fol, b2, xe_h, xe_l, end_w, gv_acc, gv_hbm),
            (inc, c2, gf_h, gf_l, from_w, out_acc, out_hbm),
        )[i]
        grad = local_maps[i]
        states = []
        for copy, d in zip([None] + x2[i], (0,) + FAR_X):
            if copy is not None:
                copy.wait_recv()
            q = lax.rem(mx + NX - d, NX)
            state2 = split(carried[q])
            states.append((q, state2))
            grad = grad + dot3((w_h[q], w_l[q]), state2, NT)
        for k in range(NH):
            rs_s[i, k] = grad[16 * k : 16 * k + 16, :]
        for copy in rs[i]:
            copy.start()
        rs_r[i, head] = rs_s[i, head]
        for n, (q, state2) in enumerate(states):
            acc_ref[q] = acc_ref[q] + weight[q] * dot3(map2, state2)
            store(i, n, acc_ref.at[q], hbm, q).start()

    def store(i, n, src, hbm, q):
        return pltpu.make_async_copy(src, hbm.at[:, pl.ds(pl.multiple_of(q * 128, 128), 128)], out_sem.at[i, n])

    @pl.when(mz == 0)
    def _():
        forward_total()
        enter[...] = jnp.zeros((128, 128), F32)
        hand_over_state()
        pl.semaphore_wait(reach, 2)
        forward_z1()
        for copy in x1[0]:
            copy.wait_recv()
        forward_x2()

    @pl.when(mz != 0)
    def _():
        backward_z1()
        forward_total()
        pl.when(mz == 1)(hand_on.wait_recv)
        pl.when(mz == 1)(hand_over_state)
        forward_z1()
        pl.when(mz == 1)(forward_x2)

    scores, scores_t = dot3(c2, b2, NT), dot3(b2, c2, NT)
    inner = jnp.zeros((128, 128), F32)
    for q in range(NX):
        cols = slice(q * 128, (q + 1) * 128)
        x, gq = scaled[q], g[:, cols]
        xv, gv2 = split(x), split(gq)
        outs, grads = [], []
        for k in range(2):
            h = 2 * q + k
            mine = first if k == 0 else jnp.logical_not(first)
            gap = column(3, h) - cum[h : h + 1, :]
            kept = jnp.exp(jnp.where(lower, gap, -gap))
            below = jnp.where(lower, kept, 0.0)
            above = jnp.where(upper, kept, 0.0)
            part = split(jnp.where(mine, gq, 0.0))
            inner = inner + dot3(part, xv, NT) * below
            outs.append(dot3(split(scores * below), xv))
            grads.append(dot3(split(scores_t * above), gv2))
        skip = jnp.where(first[0:1], gain[2 * q], gain[2 * q + 1])
        step_w = pair(0, q)
        out_acc[q] = jnp.where(first, outs[0], outs[1]) + skip * v[:, cols]
        gv_acc[q] = step_w * jnp.where(first, grads[0], grads[1]) + skip * gq
    local_maps[1] = dot3(split(inner), b2)
    local_maps[0] = dot3(split(inner.T), c2)

    for copy, d in zip(z1[0], FAR_Z):
        pl.when(lax.rem(mz + NZ - d, NZ) != 0)(copy.wait_recv)
    carry = jnp.zeros((8, 128), F32)
    for j in range(NZ - 1, -1, -1):
        ys_b[j] = carry
        if j > 0:
            carry = carry * zr_b[j, 8:9, :] + zr_b[j, 0:8, :]
    for copy in z2[0]:
        copy.start()
    leave[mine_rows, :] = ys_b[mz]

    @pl.when(mz == 2)
    def _():
        hand_on.wait_recv()
        if EARLY > 3:
            hand_over_state()
        forward_x2()

    for copy, d in zip(z1[1], FAR_Z):
        pl.when(lax.rem(mz + NZ - d, NZ) != NZ - 1)(copy.wait_recv)
    carry = zr_f[0]
    for j in range(1, NZ):
        ys_f[j] = carry
        if j < NZ - 1:
            carry = carry * zr_b[j, 8:9, :] + zr_f[j]
    for copy, d in zip(z2[1], FAR_Z):
        pl.when(lax.rem(mz + d, NZ) >= EARLY)(copy.start)

    if EARLY > 3:

        @pl.when(mz == 3)
        def _():
            hand_on.wait_recv()
            forward_x2()

    for copy in z2[0]:
        copy.wait_recv()
    backward_x2(leave[...])

    @pl.when(early)
    def _():
        last(1)

    @pl.when(jnp.logical_not(early))
    def _():
        enter[mine_rows, :] = ys_f[mz]
        for copy in z2[1]:
            copy.wait_recv()
        forward_x2()

    last(0)

    @pl.when(jnp.logical_not(early))
    def _():
        last(1)

    ends = []
    for i in (1, 0):
        for copy in rs[i]:
            copy.wait_recv()
        whole = rs_r[i, 0]
        for k in range(1, NH):
            whole = whole + rs_r[i, k]
        maps[i] = whole
        ends.append(pltpu.make_async_copy(maps.at[i], maps_hbm.at[i], out_sem.at[i, NX]))
        ends[-1].start()
    for i, (acc_ref, hbm) in enumerate(((gv_acc, gv_hbm), (out_acc, out_hbm))):
        for n in range(NX):
            store(i, n, acc_ref.at[n], hbm, n).wait()
    for copy in ends:
        copy.wait()
    for copy in z1[0]:
        pl.when(mz != 0)(copy.wait_send)
    for copy in z1[1]:
        pl.when(mz != NZ - 1)(copy.wait_send)
    for copy in x1[0] + x1[1] + z2[0] + x2[0] + x2[1] + rs[0] + rs[1]:
        copy.wait_send()
    for copy, d in zip(z2[1], FAR_Z):
        pl.when(lax.rem(mz + d, NZ) >= EARLY)(copy.wait_send)
    pl.when(mz < EARLY - 1)(hand_on.wait_send)


def hand_kernel(out_in, gv_in, maps_in, out, gv, gi, go, wide, small, sem):
    pairs = (
        (out_in, wide.at[0], out), (gv_in, wide.at[1], gv), (maps_in.at[0], small.at[0], gi), (maps_in.at[1], small.at[1], go)
    )
    loads = [pltpu.make_async_copy(src, via, sem.at[0, i]) for i, (src, via, _) in enumerate(pairs)]
    stores = [pltpu.make_async_copy(via, dst, sem.at[1, i]) for i, (_, via, dst) in enumerate(pairs)]
    for copy in loads:
        copy.start()
    for load, store in zip(loads, stores):
        load.wait()
        store.start()
    for copy in stores:
        copy.wait()


def shards(values, step_size, decay_rate, input_map, output_map, skip_gain, grad_output):
    far = pl.BlockSpec(memory_space=pltpu.HBM)
    vmem = lambda *shape, dtype=F32: pltpu.VMEM(shape, dtype)
    dma = lambda *shape: pltpu.SemaphoreType.DMA(shape)
    full = jax.ShapeDtypeStruct(values.shape, F32)
    out, gv, maps = pl.pallas_call(
        core_kernel,
        name="scan_core",
        out_shape=(full, full, jax.ShapeDtypeStruct((2, 16, 128), F32)),
        in_specs=[far] * 7,
        out_specs=(far,) * 3,
        scratch_shapes=[
            vmem(128, 512), vmem(128, 512), vmem(8, 128), vmem(128, 128), vmem(128, 128),
            pltpu.SMEM((8,), F32), pltpu.SMEM((8,), F32),
            vmem(4, 128, 128), vmem(4, 128, 128), vmem(2, 16, 128), vmem(4, 128, 128), vmem(4, 128, 128),
            vmem(4, 128, 128, dtype=BF16), vmem(4, 128, 128, dtype=BF16),
            vmem(4, 128, 128, dtype=BF16), vmem(4, 128, 128, dtype=BF16), vmem(2, 128, 128),
            vmem(4, 129, 128), vmem(4, 129, 128), vmem(4, 129, 128), vmem(4, 129, 128),
            vmem(16, 8, 128), vmem(16, 9, 128), vmem(16, 8, 128), vmem(16, 9, 128),
            vmem(16, 8, 128), vmem(16, 8, 128), vmem(128, 128), vmem(128, 128), vmem(128, 128), vmem(128, 128),
            vmem(4, 128, 128), vmem(4, 128, 128), vmem(4, 128, 128), vmem(4, 128, 128),
            vmem(2, 8, 16, 128), vmem(2, 8, 16, 128),
            pltpu.SemaphoreType.REGULAR, pltpu.SemaphoreType.DMA, pltpu.SemaphoreType.DMA, dma(7), dma(2, 3), dma(2, 3), dma(2, 15), dma(2, 15), dma(2, 15), dma(2, 15), dma(2, 3), dma(2, 3),
            dma(2, 7), dma(2, 7), dma(2, 5),
        ],
        compiler_params=pltpu.CompilerParams(
            collective_id=0, has_side_effects=True, vmem_limit_bytes=60 * 1024 * 1024
        ),
    )(values, step_size, decay_rate, input_map, output_map, skip_gain, grad_output)
    piece = jax.ShapeDtypeStruct((16, 128), F32)
    return pl.pallas_call(
        hand_kernel,
        name="hand_over",
        out_shape=(full, full, piece, piece),
        in_specs=[far] * 3,
        out_specs=(far,) * 4,
        scratch_shapes=[vmem(2, 128, 512), vmem(2, 16, 128), dma(2, 4)],
    )(out, gv, maps)


def solution(mesh):
    placed = (
        P("ctx", "head"),
        P("head", "ctx"),
        P("head"),
        P("ctx", None),
        P("ctx", None),
        P("head"),
        P("ctx", "head"),
    )
    return jax.shard_map(
        shards,
        mesh=mesh,
        in_specs=placed,
        out_specs=(
            P("ctx", "head"),
            P("ctx", "head"),
            P(("ctx", "head"), None),
            P(("ctx", "head"), None),
        ),
        check_vma=False,
    )
```

```python
import functools

import jax
import jax.numpy as jnp
from jax import lax
from jax.experimental import pallas as pl
from jax.experimental.pallas import tpu as pltpu
from jax.sharding import PartitionSpec as P

MESH = pl.DeviceIdType.MESH
F32, BF16 = jnp.float32, jnp.bfloat16
NX, NZ, NH = 4, 16, 8
EARLY = 4
FAR_Z = (8, 7, 9, 6, 10, 5, 11, 4, 12, 3, 13, 2, 14, 1, 15)
NEAR_Z = (4, 12, 3, 13, 2, 14, 1, 15)
FAR_X = (2, 1, 3)
FAR_H = (4, 5, 3, 6, 2, 7, 1)
NN = (((1,), (0,)), ((), ()))
NT = (((1,), (1,)), ((), ()))


def split(x):
    high = x.astype(BF16)
    return high, (x - high.astype(F32)).astype(BF16)


def dot3(a, b, dims=NN):
    (ah, al), (bh, bl) = a, b
    one = functools.partial(lax.dot_general, dimension_numbers=dims, preferred_element_type=F32)
    return one(ah, bh) + (one(al, bh) + one(ah, bl))


def core_kernel(
    v_hbm, step_hbm, rate_hbm, b_hbm, c_hbm, gain_hbm, g_hbm,
    out_hbm, gv_hbm, rs_r,
    v, g, step, bmap, cmap, rate, gain,
    out_acc, gv_acc, from_w, end_w, gf_h, gf_l, xe_h, xe_l, local_maps,
    xs_f, xs_b, xr_f, xr_b, zs_f, zs_b, zr_f, zr_b, ys_f, ys_b, enter, leave, handed, total_f, ws_f, ws_b, inc, fol, rs_s,
    reach, hand_s, hand_r, load_sem, x1_s, x1_r, z1_s, z1_r, z2_s, z2_r, x2_s, x2_r, rs_ss, rs_rs, out_sem,
):
    ctx, head = lax.axis_index("ctx"), lax.axis_index("head")
    mz, mx = ctx // NX, ctx % NX

    def at_x(d):
        return (mz * NX + lax.rem(mx + d, NX), head)

    def at_z(d):
        return (lax.rem(mz + d, NZ) * NX + mx, head)

    def at_h(d):
        return (ctx, lax.rem(head + d, NH))

    barrier = pltpu.get_barrier_semaphore()
    partners = [at_z(d) for d in NEAR_Z] + [at_h(d) for d in FAR_H] + [at_x(d) for d in FAR_X]
    for partner in partners:
        pl.semaphore_signal(barrier, inc=1, device_id=partner, device_id_type=MESH)

    loads = [
        pltpu.make_async_copy(src, dst, load_sem.at[i])
        for i, (src, dst) in enumerate(
            ((step_hbm, step), (rate_hbm, rate), (b_hbm, bmap), (c_hbm, cmap), (v_hbm, v), (g_hbm, g), (gain_hbm, gain))
        )
    ]
    for load in loads:
        load.start()

    rows = lax.broadcasted_iota(jnp.int32, (128, 128), 0)
    lanes = lax.broadcasted_iota(jnp.int32, (128, 128), 1)
    first = lanes < 64
    lower = rows >= lanes
    upper = rows <= lanes

    loads[0].wait()
    loads[1].wait()
    steps = step[...]
    head_rows = lax.broadcasted_iota(jnp.int32, (NH, 128), 0)
    rates = jnp.zeros((NH, 128), F32)
    for h in range(NH):
        rates = jnp.where(head_rows == h, rate[h], rates)
    cum = lax.dot_general(
        steps * rates, jnp.where(upper, 1.0, 0.0).astype(F32), NN,
        precision=lax.Precision.HIGHEST, preferred_element_type=F32,
    )
    total = cum[:, 127:128]
    table = jnp.concatenate([steps, jnp.exp(cum), jnp.exp(total - cum), cum] + [jnp.zeros((96, 128), F32)], axis=0)
    table = table.T

    def column(kind, h):
        k = kind * NH + h
        return jnp.broadcast_to(table[:, k : k + 1], (128, 128))

    def pair(kind, q):
        return jnp.where(first, column(kind, 2 * q), column(kind, 2 * q + 1))

    loads[2].wait()
    loads[3].wait()
    b_all, c_all = bmap[...], cmap[...]
    b2, c2 = split(b_all), split(c_all)
    bt2, ct2 = split(b_all.T), split(c_all.T)
    loads[4].wait()
    loads[5].wait()
    loads[6].wait()

    scaled = []
    for q in range(NX):
        cols = slice(q * 128, (q + 1) * 128)
        step_w, start, end = pair(0, q), pair(1, q), pair(2, q)
        vq, gq = v[:, cols], g[:, cols]
        x = vq * step_w
        scaled.append(x)
        xe, gf = split(x * end), split(gq * start)
        xe_h[q], xe_l[q] = xe
        gf_h[q], gf_l[q] = gf
        from_w[q] = start
        end_w[q] = end * step_w
        xs_b[q, 0:128, :] = dot3(ct2, gf)
        xs_b[q, 128:129, :] = start[127:128, :]
        xs_f[q, 0:128, :] = dot3(bt2, xe)
        xs_f[q, 128:129, :] = start[127:128, :]

    pl.semaphore_wait(barrier, len(partners))
    for d in (4, 12):
        pl.semaphore_signal(reach, inc=1, device_id=at_z(d), device_id_type=MESH)

    def remote(src, dst, send_sem, recv_sem, partner):
        return pltpu.make_async_remote_copy(
            src_ref=src, dst_ref=dst, send_sem=send_sem, recv_sem=recv_sem, device_id=partner, device_id_type=MESH
        )

    mine_rows = pl.ds(pl.multiple_of(mz * 8, 8), 8)
    xs, xr, zs, zr, ys, carried_in = (xs_b, xs_f), (xr_b, xr_f), (zs_b, zs_f), (zr_b, zr_f), (ys_b, ys_f), (leave, enter)
    ws, states_in = (ws_b, ws_f), (fol, inc)
    x1 = [[
        remote(xs[i].at[lax.rem(mx + d, NX)], xr[i].at[mx], x1_s.at[i, d - 1], x1_r.at[i, d - 1], at_x(d)) for d in FAR_X
    ] for i in range(2)]
    z1 = [[
        remote(zs[i].at[lax.rem(mz + d, NZ)], zr[i].at[mz], z1_s.at[i, d - 1], z1_r.at[i, d - 1], at_z(d)) for d in FAR_Z
    ] for i in range(2)]
    z2 = [[
        remote(
            ys[i].at[lax.rem(mz + d, NZ)], carried_in[i].at[mine_rows], z2_s.at[i, d - 1], z2_r.at[i, d - 1], at_z(d)
        ) for d in FAR_Z
    ] for i in range(2)]
    x2 = [[
        remote(ws[i].at[lax.rem(mx + d, NX)], states_in[i].at[mx], x2_s.at[i, d - 1], x2_r.at[i, d - 1], at_x(d))
        for d in FAR_X
    ] for i in range(2)]
    rs = [[
        remote(rs_s.at[i, lax.rem(head + d, NH)], rs_r.at[i, head], rs_ss.at[i, d - 1], rs_rs.at[i, d - 1], at_h(d))
        for d in FAR_H
    ] for i in range(2)]

    def x1_send(i):
        for copy in x1[i]:
            copy.start()

    @pl.when(mz == 0)
    def _():
        x1_send(1)
        x1_send(0)

    @pl.when(mz != 0)
    def _():
        x1_send(0)
        x1_send(1)

    for i in range(2):
        xr[i][mx] = xs[i][mx]

    def decay(i, k):
        return xr[i][k, 128:129, :]

    def backward_z1():
        for copy in x1[0]:
            copy.wait_recv()
        acc = xr_b[NX - 1, 0:128, :]
        for k in range(NX - 2, -1, -1):
            acc = acc * decay(0, k) + xr_b[k, 0:128, :]
        plane = decay(0, 0) * decay(0, 1) * decay(0, 2) * decay(0, 3)
        for j in range(NZ):
            zs_b[j, 0:8, :] = acc[8 * j : 8 * j + 8, :]
            zs_b[j, 8:9, :] = plane
        pl.semaphore_wait(reach, 2)
        for copy in z1[0]:
            copy.start()
        zr_b[mz] = zs_b[mz]

    def forward_total():
        for copy in x1[1]:
            copy.wait_recv()
        acc = xr_f[0, 0:128, :]
        for k in range(1, NX):
            acc = acc * decay(1, k) + xr_f[k, 0:128, :]
        total_f[...] = acc
        for j in range(NZ):
            zs_f[j] = acc[8 * j : 8 * j + 8, :]

    def forward_z1():
        for copy in z1[1]:
            pl.when(mz != NZ - 1)(copy.start)
        zr_f[mz] = zs_f[mz]

    early = mz < EARLY
    hand_on = remote(handed, enter, hand_s, hand_r, at_z(1))

    def hand_over_state():
        plane = decay(1, 0) * decay(1, 1) * decay(1, 2) * decay(1, 3)
        handed[...] = enter[...] * plane + total_f[...]
        hand_on.start()

    def forward_x2():
        carry = enter[...]
        for k in range(NX):
            ws_f[k] = carry
            if k < NX - 1:
                carry = carry * decay(1, k) + xr_f[k, 0:128, :]
        for copy in x2[1]:
            copy.start()
        inc[mx] = ws_f[mx]

    def backward_x2(carry):
        for k in range(NX - 1, -1, -1):
            ws_b[k] = carry
            if k > 0:
                carry = carry * decay(0, k) + xr_b[k, 0:128, :]
        for copy in x2[0]:
            copy.start()
        fol[mx] = ws_b[mx]

    def last(i):
        carried, map2, w_h, w_l, weight, acc_ref, hbm = (
            (fol, b2, xe_h, xe_l, end_w, gv_acc, gv_hbm),
            (inc, c2, gf_h, gf_l, from_w, out_acc, out_hbm),
        )[i]
        grad = local_maps[i]
        states = []
        for copy, d in zip([None] + x2[i], (0,) + FAR_X):
            if copy is not None:
                copy.wait_recv()
            q = lax.rem(mx + NX - d, NX)
            state2 = split(carried[q])
            states.append((q, state2))
            grad = grad + dot3((w_h[q], w_l[q]), state2, NT)
        for k in range(NH):
            rs_s[i, k] = grad[16 * k : 16 * k + 16, :]
        for copy in rs[i]:
            copy.start()
        own_piece(i).start()
        for n, (q, state2) in enumerate(states):
            acc_ref[q] = acc_ref[q] + weight[q] * dot3(map2, state2)
            store(i, n, acc_ref.at[q], hbm, q).start()

    def own_piece(i):
        return pltpu.make_async_copy(rs_s.at[i, head], rs_r.at[i, head], out_sem.at[i, NX])

    def store(i, n, src, hbm, q):
        return pltpu.make_async_copy(src, hbm.at[:, pl.ds(pl.multiple_of(q * 128, 128), 128)], out_sem.at[i, n])

    @pl.when(mz == 0)
    def _():
        forward_total()
        enter[...] = jnp.zeros((128, 128), F32)
        hand_over_state()
        pl.semaphore_wait(reach, 2)
        forward_z1()
        for copy in x1[0]:
            copy.wait_recv()
        forward_x2()

    @pl.when(mz != 0)
    def _():
        backward_z1()
        forward_total()
        pl.when(mz == 1)(hand_on.wait_recv)
        pl.when(mz == 1)(hand_over_state)
        forward_z1()
        pl.when(mz == 1)(forward_x2)

    scores, scores_t = dot3(c2, b2, NT), dot3(b2, c2, NT)
    inner = jnp.zeros((128, 128), F32)
    for q in range(NX):
        cols = slice(q * 128, (q + 1) * 128)
        x, gq = scaled[q], g[:, cols]
        xv, gv2 = split(x), split(gq)
        outs, grads = [], []
        for k in range(2):
            h = 2 * q + k
            mine = first if k == 0 else jnp.logical_not(first)
            gap = column(3, h) - cum[h : h + 1, :]
            kept = jnp.exp(jnp.where(lower, gap, -gap))
            below = jnp.where(lower, kept, 0.0)
            above = jnp.where(upper, kept, 0.0)
            part = split(jnp.where(mine, gq, 0.0))
            inner = inner + dot3(part, xv, NT) * below
            outs.append(dot3(split(scores * below), xv))
            grads.append(dot3(split(scores_t * above), gv2))
        skip = jnp.where(first[0:1], gain[2 * q], gain[2 * q + 1])
        step_w = pair(0, q)
        out_acc[q] = jnp.where(first, outs[0], outs[1]) + skip * v[:, cols]
        gv_acc[q] = step_w * jnp.where(first, grads[0], grads[1]) + skip * gq
    local_maps[1] = dot3(split(inner), b2)
    local_maps[0] = dot3(split(inner.T), c2)

    for copy, d in zip(z1[0], FAR_Z):
        pl.when(lax.rem(mz + NZ - d, NZ) != 0)(copy.wait_recv)
    carry = jnp.zeros((8, 128), F32)
    for j in range(NZ - 1, -1, -1):
        ys_b[j] = carry
        if j > 0:
            carry = carry * zr_b[j, 8:9, :] + zr_b[j, 0:8, :]
    for copy in z2[0]:
        copy.start()
    leave[mine_rows, :] = ys_b[mz]

    @pl.when(mz == 2)
    def _():
        hand_on.wait_recv()
        if EARLY > 3:
            hand_over_state()
        forward_x2()

    for copy, d in zip(z1[1], FAR_Z):
        pl.when(lax.rem(mz + NZ - d, NZ) != NZ - 1)(copy.wait_recv)
    carry = zr_f[0]
    for j in range(1, NZ):
        ys_f[j] = carry
        if j < NZ - 1:
            carry = carry * zr_b[j, 8:9, :] + zr_f[j]
    for copy, d in zip(z2[1], FAR_Z):
        pl.when(lax.rem(mz + d, NZ) >= EARLY)(copy.start)

    if EARLY > 3:

        @pl.when(mz == 3)
        def _():
            hand_on.wait_recv()
            forward_x2()

    for copy in z2[0]:
        copy.wait_recv()
    backward_x2(leave[...])

    @pl.when(early)
    def _():
        last(1)

    @pl.when(jnp.logical_not(early))
    def _():
        enter[mine_rows, :] = ys_f[mz]
        for copy in z2[1]:
            copy.wait_recv()
        forward_x2()

    last(0)

    @pl.when(jnp.logical_not(early))
    def _():
        last(1)

    for i, (acc_ref, hbm) in enumerate(((gv_acc, gv_hbm), (out_acc, out_hbm))):
        for n in range(NX):
            store(i, n, acc_ref.at[n], hbm, n).wait()
        own_piece(i).wait()
        for copy in rs[i]:
            copy.wait_recv()
    for copy in z1[0]:
        pl.when(mz != 0)(copy.wait_send)
    for copy in z1[1]:
        pl.when(mz != NZ - 1)(copy.wait_send)
    for copy in x1[0] + x1[1] + z2[0] + x2[0] + x2[1] + rs[0] + rs[1]:
        copy.wait_send()
    for copy, d in zip(z2[1], FAR_Z):
        pl.when(lax.rem(mz + d, NZ) >= EARLY)(copy.wait_send)
    pl.when(mz < EARLY - 1)(hand_on.wait_send)


def hand_kernel(out_in, gv_in, pieces_in, out, gv, gi, go, wide, pieces, sums, sem):
    loads = [
        pltpu.make_async_copy(src, via, sem.at[0, i])
        for i, (src, via) in enumerate(((pieces_in, pieces), (out_in, wide.at[0]), (gv_in, wide.at[1])))
    ]
    stores = [
        pltpu.make_async_copy(via, dst, sem.at[1, i])
        for i, (via, dst) in enumerate(((sums.at[0], gi), (sums.at[1], go), (wide.at[0], out), (wide.at[1], gv)))
    ]
    for copy in loads:
        copy.start()
    loads[0].wait()
    for i in range(2):
        whole = pieces[i, 0]
        for k in range(1, NH):
            whole = whole + pieces[i, k]
        sums[i] = whole
        stores[i].start()
    for i in range(2):
        loads[i + 1].wait()
        stores[i + 2].start()
    for copy in stores:
        copy.wait()


def shards(values, step_size, decay_rate, input_map, output_map, skip_gain, grad_output):
    far = pl.BlockSpec(memory_space=pltpu.HBM)
    vmem = lambda *shape, dtype=F32: pltpu.VMEM(shape, dtype)
    dma = lambda *shape: pltpu.SemaphoreType.DMA(shape)
    full = jax.ShapeDtypeStruct(values.shape, F32)
    out, gv, pieces = pl.pallas_call(
        core_kernel,
        name="scan_core",
        out_shape=(full, full, jax.ShapeDtypeStruct((2, NH, 16, 128), F32)),
        in_specs=[far] * 7,
        out_specs=(far,) * 3,
        scratch_shapes=[
            vmem(128, 512), vmem(128, 512), vmem(8, 128), vmem(128, 128), vmem(128, 128),
            pltpu.SMEM((8,), F32), pltpu.SMEM((8,), F32),
            vmem(4, 128, 128), vmem(4, 128, 128), vmem(4, 128, 128), vmem(4, 128, 128),
            vmem(4, 128, 128, dtype=BF16), vmem(4, 128, 128, dtype=BF16),
            vmem(4, 128, 128, dtype=BF16), vmem(4, 128, 128, dtype=BF16), vmem(2, 128, 128),
            vmem(4, 129, 128), vmem(4, 129, 128), vmem(4, 129, 128), vmem(4, 129, 128),
            vmem(16, 8, 128), vmem(16, 9, 128), vmem(16, 8, 128), vmem(16, 9, 128),
            vmem(16, 8, 128), vmem(16, 8, 128), vmem(128, 128), vmem(128, 128), vmem(128, 128), vmem(128, 128),
            vmem(4, 128, 128), vmem(4, 128, 128), vmem(4, 128, 128), vmem(4, 128, 128),
            vmem(2, 8, 16, 128),
            pltpu.SemaphoreType.REGULAR, pltpu.SemaphoreType.DMA, pltpu.SemaphoreType.DMA, dma(7), dma(2, 3), dma(2, 3), dma(2, 15), dma(2, 15), dma(2, 15), dma(2, 15), dma(2, 3), dma(2, 3),
            dma(2, 7), dma(2, 7), dma(2, 5),
        ],
        compiler_params=pltpu.CompilerParams(
            collective_id=0, has_side_effects=True, vmem_limit_bytes=60 * 1024 * 1024
        ),
    )(values, step_size, decay_rate, input_map, output_map, skip_gain, grad_output)
    piece = jax.ShapeDtypeStruct((16, 128), F32)
    return pl.pallas_call(
        hand_kernel,
        name="hand_over",
        out_shape=(full, full, piece, piece),
        in_specs=[far] * 3,
        out_specs=(far,) * 4,
        scratch_shapes=[vmem(2, 128, 512), vmem(2, 8, 16, 128), vmem(2, 16, 128), dma(2, 4)],
    )(out, gv, pieces)


def solution(mesh):
    placed = (
        P("ctx", "head"),
        P("head", "ctx"),
        P("head"),
        P("ctx", None),
        P("ctx", None),
        P("head"),
        P("ctx", "head"),
    )
    return jax.shard_map(
        shards,
        mesh=mesh,
        in_specs=placed,
        out_specs=(
            P("ctx", "head"),
            P("ctx", "head"),
            P(("ctx", "head"), None),
            P(("ctx", "head"), None),
        ),
        check_vma=False,
    )
```

```python
import functools

import jax
import jax.numpy as jnp
from jax import lax
from jax.experimental import pallas as pl
from jax.experimental.pallas import tpu as pltpu
from jax.sharding import PartitionSpec as P

MESH = pl.DeviceIdType.MESH
F32, BF16 = jnp.float32, jnp.bfloat16
NX, NZ, NH = 4, 16, 8
EARLY = 4
FAR_Z = (8, 7, 9, 6, 10, 5, 11, 4, 12, 3, 13, 2, 14, 1, 15)
NEAR_Z = (4, 12, 3, 13, 2, 14, 1, 15)
FAR_X = (2, 1, 3)
FAR_H = (4, 5, 3, 6, 2, 7, 1)
NN = (((1,), (0,)), ((), ()))
NT = (((1,), (1,)), ((), ()))


def split(x):
    high = x.astype(BF16)
    return high, (x - high.astype(F32)).astype(BF16)


def dot3(a, b, dims=NN):
    (ah, al), (bh, bl) = a, b
    one = functools.partial(lax.dot_general, dimension_numbers=dims, preferred_element_type=F32)
    return one(ah, bh) + (one(al, bh) + one(ah, bl))


def core_kernel(
    v_hbm, step_hbm, rate_hbm, b_hbm, c_hbm, gain_hbm, g_hbm,
    out_hbm, gv_hbm, rs_r,
    v, g, step, bmap, cmap, rate, gain,
    out_acc, gv_acc, from_w, end_w, gf_h, gf_l, xe_h, xe_l, local_maps,
    xs_f, xs_b, xr_f, xr_b, zs_f, zs_b, zr_f, zr_b, ys_f, ys_b, enter, leave, handed, total_f, ws_f, ws_b, inc, fol, rs_s,
    reach, hand_s, hand_r, load_sem, x1_s, x1_r, z1_s, z1_r, z2_s, z2_r, x2_s, x2_r, rs_ss, rs_rs, out_sem,
):
    ctx, head = lax.axis_index("ctx"), lax.axis_index("head")
    mz, mx = ctx // NX, ctx % NX

    def at_x(d):
        return (mz * NX + lax.rem(mx + d, NX), head)

    def at_z(d):
        return (lax.rem(mz + d, NZ) * NX + mx, head)

    def at_h(d):
        return (ctx, lax.rem(head + d, NH))

    barrier = pltpu.get_barrier_semaphore()
    partners = [at_z(d) for d in NEAR_Z] + [at_h(d) for d in FAR_H] + [at_x(d) for d in FAR_X]
    for partner in partners:
        pl.semaphore_signal(barrier, inc=1, device_id=partner, device_id_type=MESH)

    loads = [
        pltpu.make_async_copy(src, dst, load_sem.at[i])
        for i, (src, dst) in enumerate(
            ((step_hbm, step), (rate_hbm, rate), (b_hbm, bmap), (c_hbm, cmap), (v_hbm, v), (g_hbm, g), (gain_hbm, gain))
        )
    ]
    for load in loads:
        load.start()

    rows = lax.broadcasted_iota(jnp.int32, (128, 128), 0)
    lanes = lax.broadcasted_iota(jnp.int32, (128, 128), 1)
    first = lanes < 64
    lower = rows >= lanes
    upper = rows <= lanes

    loads[0].wait()
    loads[1].wait()
    steps = step[...]
    head_rows = lax.broadcasted_iota(jnp.int32, (NH, 128), 0)
    rates = jnp.zeros((NH, 128), F32)
    for h in range(NH):
        rates = jnp.where(head_rows == h, rate[h], rates)
    cum = lax.dot_general(
        steps * rates, jnp.where(upper, 1.0, 0.0).astype(F32), NN,
        precision=lax.Precision.HIGHEST, preferred_element_type=F32,
    )
    total = cum[:, 127:128]
    table = jnp.concatenate([steps, jnp.exp(cum), jnp.exp(total - cum), cum] + [jnp.zeros((96, 128), F32)], axis=0)
    table = table.T

    def column(kind, h):
        k = kind * NH + h
        return jnp.broadcast_to(table[:, k : k + 1], (128, 128))

    def pair(kind, q):
        return jnp.where(first, column(kind, 2 * q), column(kind, 2 * q + 1))

    loads[2].wait()
    loads[3].wait()
    b_all, c_all = bmap[...], cmap[...]
    b2, c2 = split(b_all), split(c_all)
    bt2, ct2 = split(b_all.T), split(c_all.T)
    loads[4].wait()
    loads[5].wait()
    loads[6].wait()

    scaled = []
    for q in range(NX):
        cols = slice(q * 128, (q + 1) * 128)
        step_w, start, end = pair(0, q), pair(1, q), pair(2, q)
        vq, gq = v[:, cols], g[:, cols]
        x = vq * step_w
        scaled.append(x)
        xe, gf = split(x * end), split(gq * start)
        xe_h[q], xe_l[q] = xe
        gf_h[q], gf_l[q] = gf
        from_w[q] = start
        end_w[q] = end * step_w
        xs_b[q, 8:136, :] = dot3(ct2, gf)
        xs_b[q, 0:1, :] = start[127:128, :]
        xs_f[q, 0:128, :] = dot3(bt2, xe)
        xs_f[q, 128:129, :] = start[127:128, :]

    pl.semaphore_wait(barrier, len(partners))
    for d in (4, 12):
        pl.semaphore_signal(reach, inc=1, device_id=at_z(d), device_id_type=MESH)

    def remote(src, dst, send_sem, recv_sem, partner):
        return pltpu.make_async_remote_copy(
            src_ref=src, dst_ref=dst, send_sem=send_sem, recv_sem=recv_sem, device_id=partner, device_id_type=MESH
        )

    mine_rows = pl.ds(pl.multiple_of(mz * 8, 8), 8)
    xs, xr = (xs_b, xs_f), (xr_b, xr_f)
    x1 = [[
        remote(
            xs_b.at[lax.rem(mx + d, NX), part], xr_b.at[mx, part], x1_s.at[h, d - 1], x1_r.at[h, d - 1], at_x(d)
        ) for d in FAR_X
    ] for h, part in enumerate((slice(0, 72), slice(72, 136)))]
    x1.append([
        remote(xs_f.at[lax.rem(mx + d, NX)], xr_f.at[mx], x1_s.at[2, d - 1], x1_r.at[2, d - 1], at_x(d)) for d in FAR_X
    ])
    back_rows = pl.ds(pl.multiple_of(mz // 2 * 8 + mz % 2 * 64, 8), 8)

    def half_copies(make, parity):
        copies = []
        for m in (4, 3, 5, 2, 6, 1, 7, 0):
            d = 2 * m + parity
            copies.append((d, make(d, lax.max(d, 1) - 1)))
        return copies

    z1b = [half_copies(
        lambda d, n: remote(zs_b.at[lax.rem(mz + d, NZ)], zr_b.at[mz], z1_s.at[0, n], z1_r.at[0, n], at_z(d)), (mz + h) % 2
    ) for h in range(2)]
    z1b_in = [half_copies(
        lambda d, n: remote(zs_b.at[0], zr_b.at[0], z1_s.at[0, n], z1_r.at[0, n], at_z(d)), (mz + h) % 2
    ) for h in range(2)]
    z2b = [remote(
        ys_b.at[lax.rem(mz + d, NZ)], leave.at[back_rows], z2_s.at[0, d - 1], z2_r.at[0, d - 1], at_z(d)
    ) for d in FAR_Z]
    z2b_in = [half_copies(
        lambda d, n: remote(ys_b.at[0], leave.at[back_rows], z2_s.at[0, n], z2_r.at[0, n], at_z(d)), (mz + h) % 2
    ) for h in range(2)]
    z1 = [
        remote(zs_f.at[lax.rem(mz + d, NZ)], zr_f.at[mz], z1_s.at[1, d - 1], z1_r.at[1, d - 1], at_z(d)) for d in FAR_Z
    ]
    z2 = [
        remote(ys_f.at[lax.rem(mz + d, NZ)], enter.at[mine_rows], z2_s.at[1, d - 1], z2_r.at[1, d - 1], at_z(d))
        for d in FAR_Z
    ]
    x2 = [[
        remote(ws_b.at[lax.rem(mx + d, NX), part], fol.at[mx, part], x2_s.at[h, d - 1], x2_r.at[h, d - 1], at_x(d))
        for d in FAR_X
    ] for h, part in enumerate((slice(0, 64), slice(64, 128)))]
    x2.append([
        remote(ws_f.at[lax.rem(mx + d, NX)], inc.at[mx], x2_s.at[2, d - 1], x2_r.at[2, d - 1], at_x(d)) for d in FAR_X
    ])
    x2_out = []
    for h, part in enumerate((slice(0, 64), slice(64, 128), slice(0, 128))):
        src, dst, outs = (ws_b, ws_b, ws_f)[h], (fol, fol, inc)[h], []
        for t in (0, 1, 3, 2):
            n = lax.rem(t + NX - 1 - mx + NX, NX)
            outs.append((t, remote(
                src.at[t, part], dst.at[mx, part], x2_s.at[h, lax.min(n, 2)], x2_r.at[h, lax.min(n, 2)],
                (mz * NX + t, head),
            )))
        x2_out.append(outs)
    rs = [[
        remote(rs_s.at[i, lax.rem(head + d, NH)], rs_r.at[i, head], rs_ss.at[i, d - 1], rs_rs.at[i, d - 1], at_h(d))
        for d in FAR_H
    ] for i in range(2)]

    def x1_send(i):
        for copy in x1[i]:
            copy.start()

    @pl.when(mz == 0)
    def _():
        x1_send(2)
        x1_send(0)
        x1_send(1)

    @pl.when(mz != 0)
    def _():
        x1_send(0)
        x1_send(1)
        x1_send(2)

    for i in range(2):
        xr[i][mx] = xs[i][mx]

    def decay(i, k):
        return xr_b[k, 0:1, :] if i == 0 else xr_f[k, 128:129, :]

    def backward_z1():
        for h in range(2):
            for copy in x1[h]:
                copy.wait_recv()
            rows_in = slice(8 + 64 * h, 72 + 64 * h)
            acc = xr_b[NX - 1, rows_in, :]
            for k in range(NX - 2, -1, -1):
                acc = acc * decay(0, k) + xr_b[k, rows_in, :]
            plane = decay(0, 0) * decay(0, 1) * decay(0, 2) * decay(0, 3)
            for j in range(NZ // 2):
                zs_b[2 * j + h, 0:8, :] = acc[8 * j : 8 * j + 8, :]
                zs_b[2 * j + h, 8:9, :] = plane
            if h == 0:
                pl.semaphore_wait(reach, 2)
            for d, copy in z1b[h][:-1]:
                copy.start()
            d, copy = z1b[h][-1]
            pl.when(d != 0)(copy.start)
        zr_b[mz] = zs_b[mz]

    def forward_total():
        for copy in x1[2]:
            copy.wait_recv()
        acc = xr_f[0, 0:128, :]
        for k in range(1, NX):
            acc = acc * decay(1, k) + xr_f[k, 0:128, :]
        total_f[...] = acc
        for j in range(NZ):
            zs_f[j] = acc[8 * j : 8 * j + 8, :]

    def forward_z1():
        for copy in z1:
            pl.when(mz != NZ - 1)(copy.start)
        zr_f[mz] = zs_f[mz]

    early = mz < EARLY
    hand_on = remote(handed, enter, hand_s, hand_r, at_z(1))

    def hand_over_state():
        plane = decay(1, 0) * decay(1, 1) * decay(1, 2) * decay(1, 3)
        handed[...] = enter[...] * plane + total_f[...]
        hand_on.start()

    def forward_x2():
        carry = enter[...]
        for k in range(NX):
            ws_f[k] = carry
            if k < NX - 1:
                carry = carry * decay(1, k) + xr_f[k, 0:128, :]
        for t, copy in x2_out[2]:
            pl.when(mx != t)(copy.start)
        inc[mx] = ws_f[mx]

    def backward_x2(h):
        part, rows_in = slice(64 * h, 64 * h + 64), slice(8 + 64 * h, 72 + 64 * h)
        carry = leave[part, :]
        for k in range(NX - 1, -1, -1):
            ws_b[k, part, :] = carry
            if k > 0:
                carry = carry * decay(0, k) + xr_b[k, rows_in, :]
        for t, copy in x2_out[h]:
            pl.when(mx != t)(copy.start)
        fol[mx, part, :] = ws_b[mx, part, :]

    def last(i):
        carried, map2, w_h, w_l, weight, acc_ref, hbm = (
            (fol, b2, xe_h, xe_l, end_w, gv_acc, gv_hbm),
            (inc, c2, gf_h, gf_l, from_w, out_acc, out_hbm),
        )[i]
        grad = local_maps[i]
        states = []
        for n, d in enumerate((0,) + FAR_X):
            if d > 0:
                for copies in (x2[:2], x2[2:])[i]:
                    copies[n - 1].wait_recv()
            q = lax.rem(mx + NX - d, NX)
            state2 = split(carried[q])
            states.append((q, state2))
            grad = grad + dot3((w_h[q], w_l[q]), state2, NT)
        for k in range(NH):
            rs_s[i, k] = grad[16 * k : 16 * k + 16, :]
        for t in (1, 0, 3, 2, 5, 7, 4, 6):
            n = lax.min(lax.rem(t + 2 * NH - 1 - head, NH), NH - 2)
            copy = remote(rs_s.at[i, t], rs_r.at[i, head], rs_ss.at[i, n], rs_rs.at[i, n], (ctx, t))
            pl.when(head != t)(copy.start)
        own_piece(i).start()
        for n, (q, state2) in enumerate(states):
            acc_ref[q] = acc_ref[q] + weight[q] * dot3(map2, state2)
            store(i, n, acc_ref.at[q], hbm, q).start()

    def own_piece(i):
        return pltpu.make_async_copy(rs_s.at[i, head], rs_r.at[i, head], out_sem.at[i, NX])

    def store(i, n, src, hbm, q):
        return pltpu.make_async_copy(src, hbm.at[:, pl.ds(pl.multiple_of(q * 128, 128), 128)], out_sem.at[i, n])

    @pl.when(mz == 0)
    def _():
        forward_total()
        enter[...] = jnp.zeros((128, 128), F32)
        hand_over_state()
        pl.semaphore_wait(reach, 2)
        forward_z1()
        for copy in x1[0] + x1[1]:
            copy.wait_recv()
        forward_x2()

    @pl.when(mz != 0)
    def _():
        backward_z1()
        forward_total()
        pl.when(mz == 1)(hand_on.wait_recv)
        pl.when(mz == 1)(hand_over_state)
        forward_z1()
        pl.when(mz == 1)(forward_x2)

    scores, scores_t = dot3(c2, b2, NT), dot3(b2, c2, NT)
    inner = jnp.zeros((128, 128), F32)
    for q in range(NX):
        cols = slice(q * 128, (q + 1) * 128)
        x, gq = scaled[q], g[:, cols]
        xv, gv2 = split(x), split(gq)
        outs, grads = [], []
        for k in range(2):
            h = 2 * q + k
            mine = first if k == 0 else jnp.logical_not(first)
            gap = column(3, h) - cum[h : h + 1, :]
            kept = jnp.exp(jnp.where(lower, gap, -gap))
            below = jnp.where(lower, kept, 0.0)
            above = jnp.where(upper, kept, 0.0)
            part = split(jnp.where(mine, gq, 0.0))
            inner = inner + dot3(part, xv, NT) * below
            outs.append(dot3(split(scores * below), xv))
            grads.append(dot3(split(scores_t * above), gv2))
        skip = jnp.where(first[0:1], gain[2 * q], gain[2 * q + 1])
        step_w = pair(0, q)
        out_acc[q] = jnp.where(first, outs[0], outs[1]) + skip * v[:, cols]
        gv_acc[q] = step_w * jnp.where(first, grads[0], grads[1]) + skip * gq
    local_maps[1] = dot3(split(inner), b2)
    local_maps[0] = dot3(split(inner.T), c2)

    for h in range(2):
        for d, copy in z1b_in[h]:
            pl.when(jnp.logical_and(d != 0, lax.rem(mz + NZ - d, NZ) != 0))(copy.wait_recv)
    carry = jnp.zeros((8, 128), F32)
    for j in range(NZ - 1, -1, -1):
        ys_b[j] = carry
        if j > 0:
            carry = carry * zr_b[j, 8:9, :] + zr_b[j, 0:8, :]
    for t in (0, 1, 2, 3, 4, 5, 6, 7, 15, 14, 13, 12, 8, 11, 10, 9):
        n = lax.min(lax.rem(t + 2 * NZ - 1 - mz, NZ), NZ - 2)
        copy = remote(ys_b.at[t], leave.at[back_rows], z2_s.at[0, n], z2_r.at[0, n], (t * NX + mx, head))
        pl.when(mz != t)(copy.start)
    leave[back_rows, :] = ys_b[mz]

    @pl.when(mz == 2)
    def _():
        hand_on.wait_recv()
        if EARLY > 3:
            hand_over_state()
        forward_x2()

    for copy, d in zip(z1, FAR_Z):
        pl.when(lax.rem(mz + NZ - d, NZ) != NZ - 1)(copy.wait_recv)
    carry = zr_f[0]
    for j in range(1, NZ):
        ys_f[j] = carry
        if j < NZ - 1:
            carry = carry * zr_b[j, 8:9, :] + zr_f[j]
    for copy, d in zip(z2, FAR_Z):
        pl.when(lax.rem(mz + d, NZ) >= EARLY)(copy.start)

    if EARLY > 3:

        @pl.when(mz == 3)
        def _():
            hand_on.wait_recv()
            forward_x2()

    for h in range(2):
        for d, copy in z2b_in[h][:-1]:
            copy.wait_recv()
        d, copy = z2b_in[h][-1]
        pl.when(d != 0)(copy.wait_recv)
        backward_x2(h)

    @pl.when(early)
    def _():
        last(1)

    @pl.when(jnp.logical_not(early))
    def _():
        enter[mine_rows, :] = ys_f[mz]
        for copy in z2:
            copy.wait_recv()
        forward_x2()

    last(0)

    @pl.when(jnp.logical_not(early))
    def _():
        last(1)

    for i, (acc_ref, hbm) in enumerate(((gv_acc, gv_hbm), (out_acc, out_hbm))):
        for n in range(NX):
            store(i, n, acc_ref.at[n], hbm, n).wait()
        own_piece(i).wait()
        for copy in rs[i]:
            copy.wait_recv()
    for h in range(2):
        for d, copy in z1b[h]:
            pl.when(jnp.logical_and(mz != 0, d != 0))(copy.wait_send)
    for copy in z1:
        pl.when(mz != NZ - 1)(copy.wait_send)
    for copy in sum(x1 + x2 + rs, []) + z2b:
        copy.wait_send()
    for copy, d in zip(z2, FAR_Z):
        pl.when(lax.rem(mz + d, NZ) >= EARLY)(copy.wait_send)
    pl.when(mz < EARLY - 1)(hand_on.wait_send)


def hand_kernel(out_in, gv_in, pieces_in, out, gv, gi, go, wide, pieces, sums, sem):
    loads = [
        pltpu.make_async_copy(src, via, sem.at[0, i])
        for i, (src, via) in enumerate(((pieces_in, pieces), (out_in, wide.at[0]), (gv_in, wide.at[1])))
    ]
    stores = [
        pltpu.make_async_copy(via, dst, sem.at[1, i])
        for i, (via, dst) in enumerate(((sums.at[0], gi), (sums.at[1], go), (wide.at[0], out), (wide.at[1], gv)))
    ]
    for copy in loads:
        copy.start()
    loads[0].wait()
    for i in range(2):
        whole = pieces[i, 0]
        for k in range(1, NH):
            whole = whole + pieces[i, k]
        sums[i] = whole
        stores[i].start()
    for i in range(2):
        loads[i + 1].wait()
        stores[i + 2].start()
    for copy in stores:
        copy.wait()


def shards(values, step_size, decay_rate, input_map, output_map, skip_gain, grad_output):
    far = pl.BlockSpec(memory_space=pltpu.HBM)
    vmem = lambda *shape, dtype=F32: pltpu.VMEM(shape, dtype)
    dma = lambda *shape: pltpu.SemaphoreType.DMA(shape)
    full = jax.ShapeDtypeStruct(values.shape, F32)
    out, gv, pieces = pl.pallas_call(
        core_kernel,
        name="scan_core",
        out_shape=(full, full, jax.ShapeDtypeStruct((2, NH, 16, 128), F32)),
        in_specs=[far] * 7,
        out_specs=(far,) * 3,
        scratch_shapes=[
            vmem(128, 512), vmem(128, 512), vmem(8, 128), vmem(128, 128), vmem(128, 128),
            pltpu.SMEM((8,), F32), pltpu.SMEM((8,), F32),
            vmem(4, 128, 128), vmem(4, 128, 128), vmem(4, 128, 128), vmem(4, 128, 128),
            vmem(4, 128, 128, dtype=BF16), vmem(4, 128, 128, dtype=BF16),
            vmem(4, 128, 128, dtype=BF16), vmem(4, 128, 128, dtype=BF16), vmem(2, 128, 128),
            vmem(4, 129, 128), vmem(4, 136, 128), vmem(4, 129, 128), vmem(4, 136, 128),
            vmem(16, 8, 128), vmem(16, 9, 128), vmem(16, 8, 128), vmem(16, 9, 128),
            vmem(16, 8, 128), vmem(16, 8, 128), vmem(128, 128), vmem(128, 128), vmem(128, 128), vmem(128, 128),
            vmem(4, 128, 128), vmem(4, 128, 128), vmem(4, 128, 128), vmem(4, 128, 128),
            vmem(2, 8, 16, 128),
            pltpu.SemaphoreType.REGULAR, pltpu.SemaphoreType.DMA, pltpu.SemaphoreType.DMA, dma(7), dma(3, 3), dma(3, 3), dma(2, 15), dma(2, 15), dma(2, 15), dma(2, 15), dma(3, 3), dma(3, 3),
            dma(2, 7), dma(2, 7), dma(2, 5),
        ],
        compiler_params=pltpu.CompilerParams(
            collective_id=0, has_side_effects=True, vmem_limit_bytes=60 * 1024 * 1024
        ),
    )(values, step_size, decay_rate, input_map, output_map, skip_gain, grad_output)
    piece = jax.ShapeDtypeStruct((16, 128), F32)
    return pl.pallas_call(
        hand_kernel,
        name="hand_over",
        out_shape=(full, full, piece, piece),
        in_specs=[far] * 3,
        out_specs=(far,) * 4,
        scratch_shapes=[vmem(2, 128, 512), vmem(2, 8, 16, 128), vmem(2, 16, 128), dma(2, 4)],
    )(out, gv, pieces)


def solution(mesh):
    placed = (
        P("ctx", "head"),
        P("head", "ctx"),
        P("head"),
        P("ctx", None),
        P("ctx", None),
        P("head"),
        P("ctx", "head"),
    )
    return jax.shard_map(
        shards,
        mesh=mesh,
        in_specs=placed,
        out_specs=(
            P("ctx", "head"),
            P("ctx", "head"),
            P(("ctx", "head"), None),
            P(("ctx", "head"), None),
        ),
        check_vma=False,
    )
```

```python
import functools

import jax
import jax.numpy as jnp
from jax import lax
from jax.experimental import pallas as pl
from jax.experimental.pallas import tpu as pltpu
from jax.sharding import PartitionSpec as P

MESH = pl.DeviceIdType.MESH
F32, BF16 = jnp.float32, jnp.bfloat16
NX, NZ, NH = 4, 16, 8
EARLY = 4
FAR_Z = (8, 7, 9, 6, 10, 5, 11, 4, 12, 3, 13, 2, 14, 1, 15)
NEAR_Z = (4, 12, 3, 13, 2, 14, 1, 15)
FAR_X = (2, 1, 3)
FAR_H = (4, 5, 3, 6, 2, 7, 1)
NN = (((1,), (0,)), ((), ()))
NT = (((1,), (1,)), ((), ()))


def split(x):
    high = x.astype(BF16)
    return high, (x - high.astype(F32)).astype(BF16)


def dot3(a, b, dims=NN):
    (ah, al), (bh, bl) = a, b
    one = functools.partial(lax.dot_general, dimension_numbers=dims, preferred_element_type=F32)
    return one(ah, bh) + (one(al, bh) + one(ah, bl))


def core_kernel(
    v_hbm, step_hbm, rate_hbm, b_hbm, c_hbm, gain_hbm, g_hbm,
    out_hbm, gv_hbm, rs_r,
    v, g, step, bmap, cmap, rate, gain,
    out_acc, gv_acc, from_w, end_w, gf_h, gf_l, xe_h, xe_l, local_maps,
    xs_f, xs_b, xr_f, xr_b, zs_f, zs_b, zr_f, zr_b, ys_f, ys_b, enter, leave, handed, total_f, ws_f, ws_b, inc, fol, rs_s,
    reach, hand_s, hand_r, load_sem, x1_s, x1_r, z1_s, z1_r, z2_s, z2_r, x2_s, x2_r, rs_ss, rs_rs, out_sem,
):
    ctx, head = lax.axis_index("ctx"), lax.axis_index("head")
    mz, mx = ctx // NX, ctx % NX

    def at_x(d):
        return (mz * NX + lax.rem(mx + d, NX), head)

    def at_z(d):
        return (lax.rem(mz + d, NZ) * NX + mx, head)

    def at_h(d):
        return (ctx, lax.rem(head + d, NH))

    barrier = pltpu.get_barrier_semaphore()
    partners = [at_z(d) for d in NEAR_Z] + [at_h(d) for d in FAR_H] + [at_x(d) for d in FAR_X]
    for partner in partners:
        pl.semaphore_signal(barrier, inc=1, device_id=partner, device_id_type=MESH)

    loads = [
        pltpu.make_async_copy(src, dst, load_sem.at[i])
        for i, (src, dst) in enumerate(
            ((step_hbm, step), (rate_hbm, rate), (b_hbm, bmap), (c_hbm, cmap), (v_hbm, v), (g_hbm, g), (gain_hbm, gain))
        )
    ]
    for load in loads:
        load.start()

    rows = lax.broadcasted_iota(jnp.int32, (128, 128), 0)
    lanes = lax.broadcasted_iota(jnp.int32, (128, 128), 1)
    first = lanes < 64
    lower = rows >= lanes
    upper = rows <= lanes

    loads[0].wait()
    loads[1].wait()
    steps = step[...]
    head_rows = lax.broadcasted_iota(jnp.int32, (NH, 128), 0)
    rates = jnp.zeros((NH, 128), F32)
    for h in range(NH):
        rates = jnp.where(head_rows == h, rate[h], rates)
    cum = lax.dot_general(
        steps * rates, jnp.where(upper, 1.0, 0.0).astype(F32), NN,
        precision=lax.Precision.HIGHEST, preferred_element_type=F32,
    )
    total = cum[:, 127:128]
    table = jnp.concatenate([steps, jnp.exp(cum), jnp.exp(total - cum), cum] + [jnp.zeros((96, 128), F32)], axis=0)
    table = table.T

    def column(kind, h):
        k = kind * NH + h
        return jnp.broadcast_to(table[:, k : k + 1], (128, 128))

    def pair(kind, q):
        return jnp.where(first, column(kind, 2 * q), column(kind, 2 * q + 1))

    loads[2].wait()
    loads[3].wait()
    b_all, c_all = bmap[...], cmap[...]
    b2, c2 = split(b_all), split(c_all)
    bt2, ct2 = split(b_all.T), split(c_all.T)
    loads[4].wait()
    loads[5].wait()
    loads[6].wait()

    scaled = []
    for q in range(NX):
        cols = slice(q * 128, (q + 1) * 128)
        step_w, start, end = pair(0, q), pair(1, q), pair(2, q)
        vq, gq = v[:, cols], g[:, cols]
        x = vq * step_w
        scaled.append(x)
        xe, gf = split(x * end), split(gq * start)
        xe_h[q], xe_l[q] = xe
        gf_h[q], gf_l[q] = gf
        from_w[q] = start
        end_w[q] = end * step_w
        xs_b[q, 8:136, :] = dot3(ct2, gf)
        xs_b[q, 0:1, :] = start[127:128, :]
        xs_f[q, 0:128, :] = dot3(bt2, xe)
        xs_f[q, 128:129, :] = start[127:128, :]

    pl.semaphore_wait(barrier, len(partners))
    for d in (4, 12):
        pl.semaphore_signal(reach, inc=1, device_id=at_z(d), device_id_type=MESH)

    def remote(src, dst, send_sem, recv_sem, partner):
        return pltpu.make_async_remote_copy(
            src_ref=src, dst_ref=dst, send_sem=send_sem, recv_sem=recv_sem, device_id=partner, device_id_type=MESH
        )

    mine_rows = pl.ds(pl.multiple_of(mz * 8, 8), 8)
    xs, xr = (xs_b, xs_f), (xr_b, xr_f)
    x1 = [[
        remote(
            xs_b.at[lax.rem(mx + d, NX), part], xr_b.at[mx, part], x1_s.at[h, d - 1], x1_r.at[h, d - 1], at_x(d)
        ) for d in FAR_X
    ] for h, part in enumerate((slice(0, 72), slice(72, 136)))]
    x1.append([
        remote(xs_f.at[lax.rem(mx + d, NX)], xr_f.at[mx], x1_s.at[2, d - 1], x1_r.at[2, d - 1], at_x(d)) for d in FAR_X
    ])
    back_rows = pl.ds(pl.multiple_of(mz // 2 * 8 + mz % 2 * 64, 8), 8)

    def half_copies(make, parity):
        copies = []
        for m in (4, 3, 5, 2, 6, 1, 7, 0):
            d = 2 * m + parity
            copies.append((d, make(d, lax.max(d, 1) - 1)))
        return copies

    z1b = [half_copies(
        lambda d, n: remote(zs_b.at[lax.rem(mz + d, NZ)], zr_b.at[mz], z1_s.at[0, n], z1_r.at[0, n], at_z(d)), (mz + h) % 2
    ) for h in range(2)]
    z1b_in = [half_copies(
        lambda d, n: remote(zs_b.at[0], zr_b.at[0], z1_s.at[0, n], z1_r.at[0, n], at_z(d)), (mz + h) % 2
    ) for h in range(2)]
    z2b = [remote(
        ys_b.at[lax.rem(mz + d, NZ)], leave.at[back_rows], z2_s.at[0, d - 1], z2_r.at[0, d - 1], at_z(d)
    ) for d in FAR_Z]
    z2b_in = [half_copies(
        lambda d, n: remote(ys_b.at[0], leave.at[back_rows], z2_s.at[0, n], z2_r.at[0, n], at_z(d)), (mz + h) % 2
    ) for h in range(2)]
    z1 = [
        remote(zs_f.at[lax.rem(mz + d, NZ)], zr_f.at[mz], z1_s.at[1, d - 1], z1_r.at[1, d - 1], at_z(d)) for d in FAR_Z
    ]
    z2 = [
        remote(ys_f.at[lax.rem(mz + d, NZ)], enter.at[mine_rows], z2_s.at[1, d - 1], z2_r.at[1, d - 1], at_z(d))
        for d in FAR_Z
    ]
    x2 = [[
        remote(ws_b.at[lax.rem(mx + d, NX), part], fol.at[mx, part], x2_s.at[h, d - 1], x2_r.at[h, d - 1], at_x(d))
        for d in FAR_X
    ] for h, part in enumerate((slice(0, 64), slice(64, 128)))]
    x2.append([
        remote(ws_f.at[lax.rem(mx + d, NX)], inc.at[mx], x2_s.at[2, d - 1], x2_r.at[2, d - 1], at_x(d)) for d in FAR_X
    ])
    x2_out = []
    for h, part in enumerate((slice(0, 64), slice(64, 128), slice(0, 128))):
        src, dst, outs = (ws_b, ws_b, ws_f)[h], (fol, fol, inc)[h], []
        for t in (0, 1, 3, 2):
            n = lax.rem(t + NX - 1 - mx + NX, NX)
            outs.append((t, remote(
                src.at[t, part], dst.at[mx, part], x2_s.at[h, lax.min(n, 2)], x2_r.at[h, lax.min(n, 2)],
                (mz * NX + t, head),
            )))
        x2_out.append(outs)
    rs = [[
        remote(rs_s.at[i, lax.rem(head + d, NH)], rs_r.at[i, head], rs_ss.at[i, d - 1], rs_rs.at[i, d - 1], at_h(d))
        for d in FAR_H
    ] for i in range(2)]

    def x1_send(i):
        for copy in x1[i]:
            copy.start()

    @pl.when(mz == 0)
    def _():
        x1_send(2)
        x1_send(0)
        x1_send(1)

    @pl.when(mz != 0)
    def _():
        x1_send(0)
        x1_send(1)
        x1_send(2)

    for i in range(2):
        xr[i][mx] = xs[i][mx]

    def decay(i, k):
        return xr_b[k, 0:1, :] if i == 0 else xr_f[k, 128:129, :]

    def backward_z1():
        for h in range(2):
            for copy in x1[h]:
                copy.wait_recv()
            rows_in = slice(8 + 64 * h, 72 + 64 * h)
            acc = xr_b[NX - 1, rows_in, :]
            for k in range(NX - 2, -1, -1):
                acc = acc * decay(0, k) + xr_b[k, rows_in, :]
            plane = decay(0, 0) * decay(0, 1) * decay(0, 2) * decay(0, 3)
            for j in range(NZ // 2):
                zs_b[2 * j + h, 0:8, :] = acc[8 * j : 8 * j + 8, :]
                zs_b[2 * j + h, 8:9, :] = plane
            if h == 0:
                pl.semaphore_wait(reach, 2)
            for d, copy in z1b[h][:-1]:
                copy.start()
            d, copy = z1b[h][-1]
            pl.when(d != 0)(copy.start)
        zr_b[mz] = zs_b[mz]

    def forward_total():
        for copy in x1[2]:
            copy.wait_recv()
        acc = xr_f[0, 0:128, :]
        for k in range(1, NX):
            acc = acc * decay(1, k) + xr_f[k, 0:128, :]
        total_f[...] = acc
        for j in range(NZ):
            zs_f[j] = acc[8 * j : 8 * j + 8, :]

    def forward_z1():
        for copy in z1:
            pl.when(mz != NZ - 1)(copy.start)
        zr_f[mz] = zs_f[mz]

    early = mz < EARLY
    hand_on = remote(handed, enter, hand_s, hand_r, at_z(1))

    def hand_over_state():
        plane = decay(1, 0) * decay(1, 1) * decay(1, 2) * decay(1, 3)
        handed[...] = enter[...] * plane + total_f[...]
        hand_on.start()

    def forward_x2():
        carry = enter[...]
        for k in range(NX):
            ws_f[k] = carry
            if k < NX - 1:
                carry = carry * decay(1, k) + xr_f[k, 0:128, :]
        for t, copy in x2_out[2]:
            pl.when(mx != t)(copy.start)
        inc[mx] = ws_f[mx]

    def backward_x2(h):
        part, rows_in = slice(64 * h, 64 * h + 64), slice(8 + 64 * h, 72 + 64 * h)
        carry = leave[part, :]
        for k in range(NX - 1, -1, -1):
            ws_b[k, part, :] = carry
            if k > 0:
                carry = carry * decay(0, k) + xr_b[k, rows_in, :]
        for t, copy in x2_out[h]:
            pl.when(mx != t)(copy.start)
        fol[mx, part, :] = ws_b[mx, part, :]

    def last(i):
        carried, map2, w_h, w_l, weight, acc_ref, hbm = (
            (fol, b2, xe_h, xe_l, end_w, gv_acc, gv_hbm),
            (inc, c2, gf_h, gf_l, from_w, out_acc, out_hbm),
        )[i]
        grad = local_maps[i]
        states = []
        for d in (0, 1, 3, 2):
            if d > 0:
                for copies in (x2[:2], x2[2:])[i]:
                    copies[FAR_X.index(d)].wait_recv()
            q = lax.rem(mx + NX - d, NX)
            state2 = split(carried[q])
            states.append((q, state2))
            grad = grad + dot3((w_h[q], w_l[q]), state2, NT)
        for k in range(NH):
            rs_s[i, k] = grad[16 * k : 16 * k + 16, :]
        for t in (1, 0, 3, 2, 5, 7, 4, 6):
            n = lax.min(lax.rem(t + 2 * NH - 1 - head, NH), NH - 2)
            copy = remote(rs_s.at[i, t], rs_r.at[i, head], rs_ss.at[i, n], rs_rs.at[i, n], (ctx, t))
            pl.when(head != t)(copy.start)
        own_piece(i).start()
        for n, (q, state2) in enumerate(states):
            acc_ref[q] = acc_ref[q] + weight[q] * dot3(map2, state2)
            store(i, n, acc_ref.at[q], hbm, q).start()

    def own_piece(i):
        return pltpu.make_async_copy(rs_s.at[i, head], rs_r.at[i, head], out_sem.at[i, NX])

    def store(i, n, src, hbm, q):
        return pltpu.make_async_copy(src, hbm.at[:, pl.ds(pl.multiple_of(q * 128, 128), 128)], out_sem.at[i, n])

    @pl.when(mz == 0)
    def _():
        forward_total()
        enter[...] = jnp.zeros((128, 128), F32)
        hand_over_state()
        pl.semaphore_wait(reach, 2)
        forward_z1()
        for copy in x1[0] + x1[1]:
            copy.wait_recv()
        forward_x2()

    @pl.when(mz != 0)
    def _():
        backward_z1()
        forward_total()
        pl.when(mz == 1)(hand_on.wait_recv)
        pl.when(mz == 1)(hand_over_state)
        forward_z1()
        pl.when(mz == 1)(forward_x2)

    scores, scores_t = dot3(c2, b2, NT), dot3(b2, c2, NT)
    inner = jnp.zeros((128, 128), F32)
    for q in range(NX):
        cols = slice(q * 128, (q + 1) * 128)
        x, gq = scaled[q], g[:, cols]
        xv, gv2 = split(x), split(gq)
        outs, grads = [], []
        for k in range(2):
            h = 2 * q + k
            mine = first if k == 0 else jnp.logical_not(first)
            gap = column(3, h) - cum[h : h + 1, :]
            kept = jnp.exp(jnp.where(lower, gap, -gap))
            below = jnp.where(lower, kept, 0.0)
            above = jnp.where(upper, kept, 0.0)
            part = split(jnp.where(mine, gq, 0.0))
            inner = inner + dot3(part, xv, NT) * below
            outs.append(dot3(split(scores * below), xv))
            grads.append(dot3(split(scores_t * above), gv2))
        skip = jnp.where(first[0:1], gain[2 * q], gain[2 * q + 1])
        step_w = pair(0, q)
        out_acc[q] = jnp.where(first, outs[0], outs[1]) + skip * v[:, cols]
        gv_acc[q] = step_w * jnp.where(first, grads[0], grads[1]) + skip * gq
    local_maps[1] = dot3(split(inner), b2)
    local_maps[0] = dot3(split(inner.T), c2)

    for h in range(2):
        for d, copy in z1b_in[h]:
            pl.when(jnp.logical_and(d != 0, lax.rem(mz + NZ - d, NZ) != 0))(copy.wait_recv)
    carry = jnp.zeros((8, 128), F32)
    for j in range(NZ - 1, -1, -1):
        ys_b[j] = carry
        if j > 0:
            carry = carry * zr_b[j, 8:9, :] + zr_b[j, 0:8, :]
    for t in (0, 1, 2, 3, 4, 5, 6, 7, 15, 14, 13, 12, 8, 11, 10, 9):
        n = lax.min(lax.rem(t + 2 * NZ - 1 - mz, NZ), NZ - 2)
        copy = remote(ys_b.at[t], leave.at[back_rows], z2_s.at[0, n], z2_r.at[0, n], (t * NX + mx, head))
        pl.when(mz != t)(copy.start)
    leave[back_rows, :] = ys_b[mz]

    @pl.when(mz == 2)
    def _():
        hand_on.wait_recv()
        if EARLY > 3:
            hand_over_state()
        forward_x2()

    for copy, d in zip(z1, FAR_Z):
        pl.when(lax.rem(mz + NZ - d, NZ) != NZ - 1)(copy.wait_recv)
    carry = zr_f[0]
    for j in range(1, NZ):
        ys_f[j] = carry
        if j < NZ - 1:
            carry = carry * zr_b[j, 8:9, :] + zr_f[j]
    for copy, d in zip(z2, FAR_Z):
        pl.when(lax.rem(mz + d, NZ) >= EARLY)(copy.start)

    if EARLY > 3:

        @pl.when(mz == 3)
        def _():
            hand_on.wait_recv()
            forward_x2()

    for h in range(2):
        for d, copy in z2b_in[h][:-1]:
            copy.wait_recv()
        d, copy = z2b_in[h][-1]
        pl.when(d != 0)(copy.wait_recv)
        backward_x2(h)

    @pl.when(early)
    def _():
        last(1)

    @pl.when(jnp.logical_not(early))
    def _():
        enter[mine_rows, :] = ys_f[mz]
        for copy in z2:
            copy.wait_recv()
        forward_x2()

    last(0)

    @pl.when(jnp.logical_not(early))
    def _():
        last(1)

    for h in range(2):
        for d, copy in z1b[h]:
            pl.when(jnp.logical_and(mz != 0, d != 0))(copy.wait_send)
    for copy in z1:
        pl.when(mz != NZ - 1)(copy.wait_send)
    for copy in sum(x1 + x2, []) + z2b:
        copy.wait_send()
    for copy, d in zip(z2, FAR_Z):
        pl.when(lax.rem(mz + d, NZ) >= EARLY)(copy.wait_send)
    pl.when(mz < EARLY - 1)(hand_on.wait_send)
    for i, (acc_ref, hbm) in enumerate(((gv_acc, gv_hbm), (out_acc, out_hbm))):
        for n in range(NX):
            store(i, n, acc_ref.at[n], hbm, n).wait()
        own_piece(i).wait()
    for i in (1, 0):
        for copy in rs[i]:
            copy.wait_send()
    for i in (1, 0):
        for copy in rs[i]:
            copy.wait_recv()


def hand_kernel(out_in, gv_in, pieces_in, out, gv, gi, go, wide, pieces, sums, sem):
    loads = [
        pltpu.make_async_copy(src, via, sem.at[0, i])
        for i, (src, via) in enumerate(((pieces_in, pieces), (out_in, wide.at[0]), (gv_in, wide.at[1])))
    ]
    stores = [
        pltpu.make_async_copy(via, dst, sem.at[1, i])
        for i, (via, dst) in enumerate(((sums.at[0], gi), (sums.at[1], go), (wide.at[0], out), (wide.at[1], gv)))
    ]
    for copy in loads:
        copy.start()
    loads[0].wait()
    for i in range(2):
        whole = pieces[i, 0]
        for k in range(1, NH):
            whole = whole + pieces[i, k]
        sums[i] = whole
        stores[i].start()
    for i in range(2):
        loads[i + 1].wait()
        stores[i + 2].start()
    for copy in stores:
        copy.wait()


def shards(values, step_size, decay_rate, input_map, output_map, skip_gain, grad_output):
    far = pl.BlockSpec(memory_space=pltpu.HBM)
    vmem = lambda *shape, dtype=F32: pltpu.VMEM(shape, dtype)
    dma = lambda *shape: pltpu.SemaphoreType.DMA(shape)
    full = jax.ShapeDtypeStruct(values.shape, F32)
    out, gv, pieces = pl.pallas_call(
        core_kernel,
        name="scan_core",
        out_shape=(full, full, jax.ShapeDtypeStruct((2, NH, 16, 128), F32)),
        in_specs=[far] * 7,
        out_specs=(far,) * 3,
        scratch_shapes=[
            vmem(128, 512), vmem(128, 512), vmem(8, 128), vmem(128, 128), vmem(128, 128),
            pltpu.SMEM((8,), F32), pltpu.SMEM((8,), F32),
            vmem(4, 128, 128), vmem(4, 128, 128), vmem(4, 128, 128), vmem(4, 128, 128),
            vmem(4, 128, 128, dtype=BF16), vmem(4, 128, 128, dtype=BF16),
            vmem(4, 128, 128, dtype=BF16), vmem(4, 128, 128, dtype=BF16), vmem(2, 128, 128),
            vmem(4, 129, 128), vmem(4, 136, 128), vmem(4, 129, 128), vmem(4, 136, 128),
            vmem(16, 8, 128), vmem(16, 9, 128), vmem(16, 8, 128), vmem(16, 9, 128),
            vmem(16, 8, 128), vmem(16, 8, 128), vmem(128, 128), vmem(128, 128), vmem(128, 128), vmem(128, 128),
            vmem(4, 128, 128), vmem(4, 128, 128), vmem(4, 128, 128), vmem(4, 128, 128),
            vmem(2, 8, 16, 128),
            pltpu.SemaphoreType.REGULAR, pltpu.SemaphoreType.DMA, pltpu.SemaphoreType.DMA, dma(7), dma(3, 3), dma(3, 3), dma(2, 15), dma(2, 15), dma(2, 15), dma(2, 15), dma(3, 3), dma(3, 3),
            dma(2, 7), dma(2, 7), dma(2, 5),
        ],
        compiler_params=pltpu.CompilerParams(
            collective_id=0, has_side_effects=True, vmem_limit_bytes=60 * 1024 * 1024
        ),
    )(values, step_size, decay_rate, input_map, output_map, skip_gain, grad_output)
    piece = jax.ShapeDtypeStruct((16, 128), F32)
    return pl.pallas_call(
        hand_kernel,
        name="hand_over",
        out_shape=(full, full, piece, piece),
        in_specs=[far] * 3,
        out_specs=(far,) * 4,
        scratch_shapes=[vmem(2, 128, 512), vmem(2, 8, 16, 128), vmem(2, 16, 128), dma(2, 4)],
    )(out, gv, pieces)


def solution(mesh):
    placed = (
        P("ctx", "head"),
        P("head", "ctx"),
        P("head"),
        P("ctx", None),
        P("ctx", None),
        P("head"),
        P("ctx", "head"),
    )
    return jax.shard_map(
        shards,
        mesh=mesh,
        in_specs=placed,
        out_specs=(
            P("ctx", "head"),
            P("ctx", "head"),
            P(("ctx", "head"), None),
            P(("ctx", "head"), None),
        ),
        check_vma=False,
    )
```

```python
import functools

import jax
import jax.numpy as jnp
from jax import lax
from jax.experimental import pallas as pl
from jax.experimental.pallas import tpu as pltpu
from jax.sharding import PartitionSpec as P

MESH = pl.DeviceIdType.MESH
F32, BF16 = jnp.float32, jnp.bfloat16
NX, NZ, NH = 4, 16, 8
EARLY = 4
FAR_Z = (8, 7, 9, 6, 10, 5, 11, 4, 12, 3, 13, 2, 14, 1, 15)
NEAR_Z = (4, 12, 3, 13, 2, 14, 1, 15)
FAR_X = (2, 1, 3)
FAR_H = (4, 5, 3, 6, 2, 7, 1)
NN = (((1,), (0,)), ((), ()))
NT = (((1,), (1,)), ((), ()))


def split(x):
    high = x.astype(BF16)
    return high, (x - high.astype(F32)).astype(BF16)


def dot3(a, b, dims=NN):
    (ah, al), (bh, bl) = a, b
    one = functools.partial(lax.dot_general, dimension_numbers=dims, preferred_element_type=F32)
    return one(ah, bh) + (one(al, bh) + one(ah, bl))


def core_kernel(
    v_hbm, step_hbm, rate_hbm, b_hbm, c_hbm, gain_hbm, g_hbm,
    out_hbm, gv_hbm, rs_r,
    v, g, step, bmap, cmap, rate, gain,
    out_acc, gv_acc, from_w, end_w, gf_h, gf_l, xe_h, xe_l, local_maps,
    xs_f, xs_b, xr_f, xr_b, zs_f, zs_b, zr_f, zr_b, ys_f, ys_b, enter, leave, handed, total_f, ws_f, ws_b, inc, fol, rs_s,
    reach, hand_s, hand_r, load_sem, x1_s, x1_r, z1_s, z1_r, z2_s, z2_r, x2_s, x2_r, rs_ss, rs_rs, out_sem,
):
    ctx, head = lax.axis_index("ctx"), lax.axis_index("head")
    mz, mx = ctx // NX, ctx % NX

    def at_x(d):
        return (mz * NX + lax.rem(mx + d, NX), head)

    def at_z(d):
        return (lax.rem(mz + d, NZ) * NX + mx, head)

    def at_h(d):
        return (ctx, lax.rem(head + d, NH))

    barrier = pltpu.get_barrier_semaphore()
    partners = [at_z(d) for d in NEAR_Z] + [at_h(d) for d in FAR_H] + [at_x(d) for d in FAR_X]
    for partner in partners:
        pl.semaphore_signal(barrier, inc=1, device_id=partner, device_id_type=MESH)

    loads = [
        pltpu.make_async_copy(src, dst, load_sem.at[i])
        for i, (src, dst) in enumerate(
            ((step_hbm, step), (rate_hbm, rate), (b_hbm, bmap), (c_hbm, cmap), (v_hbm, v), (g_hbm, g), (gain_hbm, gain))
        )
    ]
    for load in loads:
        load.start()

    rows = lax.broadcasted_iota(jnp.int32, (128, 128), 0)
    lanes = lax.broadcasted_iota(jnp.int32, (128, 128), 1)
    first = lanes < 64
    lower = rows >= lanes
    upper = rows <= lanes

    loads[0].wait()
    loads[1].wait()
    steps = step[...]
    head_rows = lax.broadcasted_iota(jnp.int32, (NH, 128), 0)
    rates = jnp.zeros((NH, 128), F32)
    for h in range(NH):
        rates = jnp.where(head_rows == h, rate[h], rates)
    cum = lax.dot_general(
        steps * rates, jnp.where(upper, 1.0, 0.0).astype(F32), NN,
        precision=lax.Precision.HIGHEST, preferred_element_type=F32,
    )
    total = cum[:, 127:128]
    table = jnp.concatenate([steps, jnp.exp(cum), jnp.exp(total - cum), cum] + [jnp.zeros((96, 128), F32)], axis=0)
    table = table.T

    def column(kind, h):
        k = kind * NH + h
        return jnp.broadcast_to(table[:, k : k + 1], (128, 128))

    def pair(kind, q):
        return jnp.where(first, column(kind, 2 * q), column(kind, 2 * q + 1))

    loads[2].wait()
    loads[3].wait()
    b_all, c_all = bmap[...], cmap[...]
    b2, c2 = split(b_all), split(c_all)
    bt2, ct2 = split(b_all.T), split(c_all.T)
    loads[4].wait()
    loads[5].wait()
    loads[6].wait()

    scaled = []
    for q in range(NX):
        cols = slice(q * 128, (q + 1) * 128)
        step_w, start, end = pair(0, q), pair(1, q), pair(2, q)
        vq, gq = v[:, cols], g[:, cols]
        x = vq * step_w
        scaled.append(x)
        xe, gf = split(x * end), split(gq * start)
        xe_h[q], xe_l[q] = xe
        gf_h[q], gf_l[q] = gf
        from_w[q] = start
        end_w[q] = end * step_w
        xs_b[q, 8:136, :] = dot3(ct2, gf)
        xs_b[q, 0:1, :] = start[127:128, :]
        xs_f[q, 0:128, :] = dot3(bt2, xe)
        xs_f[q, 128:129, :] = start[127:128, :]

    pl.semaphore_wait(barrier, len(partners))
    for d in (4, 12):
        pl.semaphore_signal(reach, inc=1, device_id=at_z(d), device_id_type=MESH)

    def remote(src, dst, send_sem, recv_sem, partner):
        return pltpu.make_async_remote_copy(
            src_ref=src, dst_ref=dst, send_sem=send_sem, recv_sem=recv_sem, device_id=partner, device_id_type=MESH
        )

    mine_rows = pl.ds(pl.multiple_of(mz * 8, 8), 8)
    xs, xr = (xs_b, xs_f), (xr_b, xr_f)
    x1 = [[
        remote(
            xs_b.at[lax.rem(mx + d, NX), part], xr_b.at[mx, part], x1_s.at[h, d - 1], x1_r.at[h, d - 1], at_x(d)
        ) for d in FAR_X
    ] for h, part in enumerate((slice(0, 72), slice(72, 136)))]
    x1.append([
        remote(xs_f.at[lax.rem(mx + d, NX)], xr_f.at[mx], x1_s.at[2, d - 1], x1_r.at[2, d - 1], at_x(d)) for d in FAR_X
    ])
    back_rows = pl.ds(pl.multiple_of(mz // 2 * 8 + mz % 2 * 64, 8), 8)

    def half_copies(make, parity):
        copies = []
        for m in (4, 3, 5, 2, 6, 1, 7, 0):
            d = 2 * m + parity
            copies.append((d, make(d, lax.max(d, 1) - 1)))
        return copies

    z1b = [half_copies(
        lambda d, n: remote(zs_b.at[lax.rem(mz + d, NZ)], zr_b.at[mz], z1_s.at[0, n], z1_r.at[0, n], at_z(d)), (mz + h) % 2
    ) for h in range(2)]
    z1b_in = [half_copies(
        lambda d, n: remote(zs_b.at[0], zr_b.at[0], z1_s.at[0, n], z1_r.at[0, n], at_z(d)), (mz + h) % 2
    ) for h in range(2)]
    z2b = [remote(
        ys_b.at[lax.rem(mz + d, NZ)], leave.at[back_rows], z2_s.at[0, d - 1], z2_r.at[0, d - 1], at_z(d)
    ) for d in FAR_Z]
    z2b_in = [half_copies(
        lambda d, n: remote(ys_b.at[0], leave.at[back_rows], z2_s.at[0, n], z2_r.at[0, n], at_z(d)), (mz + h) % 2
    ) for h in range(2)]
    z1 = [
        remote(zs_f.at[lax.rem(mz + d, NZ)], zr_f.at[mz], z1_s.at[1, d - 1], z1_r.at[1, d - 1], at_z(d)) for d in FAR_Z
    ]
    z2 = [
        remote(ys_f.at[lax.rem(mz + d, NZ)], enter.at[mine_rows], z2_s.at[1, d - 1], z2_r.at[1, d - 1], at_z(d))
        for d in FAR_Z
    ]
    x2 = [[
        remote(ws_b.at[lax.rem(mx + d, NX), part], fol.at[mx, part], x2_s.at[h, d - 1], x2_r.at[h, d - 1], at_x(d))
        for d in FAR_X
    ] for h, part in enumerate((slice(0, 64), slice(64, 128)))]
    x2.append([
        remote(ws_f.at[lax.rem(mx + d, NX)], inc.at[mx], x2_s.at[2, d - 1], x2_r.at[2, d - 1], at_x(d)) for d in FAR_X
    ])
    x2_out = []
    for h, part in enumerate((slice(0, 64), slice(64, 128), slice(0, 128))):
        src, dst, outs = (ws_b, ws_b, ws_f)[h], (fol, fol, inc)[h], []
        for t in (0, 1, 3, 2):
            n = lax.rem(t + NX - 1 - mx + NX, NX)
            outs.append((t, remote(
                src.at[t, part], dst.at[mx, part], x2_s.at[h, lax.min(n, 2)], x2_r.at[h, lax.min(n, 2)],
                (mz * NX + t, head),
            )))
        x2_out.append(outs)
    rs = [[
        remote(rs_s.at[i, lax.rem(head + d, NH)], rs_r.at[i, head], rs_ss.at[i, d - 1], rs_rs.at[i, d - 1], at_h(d))
        for d in FAR_H
    ] for i in range(2)]

    def x1_send(i):
        for copy in x1[i]:
            copy.start()

    @pl.when(mz == 0)
    def _():
        x1_send(2)
        x1_send(0)
        x1_send(1)

    @pl.when(mz != 0)
    def _():
        x1_send(0)
        x1_send(1)

    for i in range(2):
        xr[i][mx] = xs[i][mx]

    def decay(i, k):
        return xr_b[k, 0:1, :] if i == 0 else xr_f[k, 128:129, :]

    def backward_z1():
        for h in range(2):
            for copy in x1[h]:
                copy.wait_recv()
            if h == 0:
                x1_send(2)
            rows_in = slice(8 + 64 * h, 72 + 64 * h)
            acc = xr_b[NX - 1, rows_in, :]
            for k in range(NX - 2, -1, -1):
                acc = acc * decay(0, k) + xr_b[k, rows_in, :]
            plane = decay(0, 0) * decay(0, 1) * decay(0, 2) * decay(0, 3)
            for j in range(NZ // 2):
                zs_b[2 * j + h, 0:8, :] = acc[8 * j : 8 * j + 8, :]
                zs_b[2 * j + h, 8:9, :] = plane
            if h == 0:
                pl.semaphore_wait(reach, 2)
            for d, copy in z1b[h][:-1]:
                copy.start()
            d, copy = z1b[h][-1]
            pl.when(d != 0)(copy.start)
        zr_b[mz] = zs_b[mz]

    def forward_total():
        for copy in x1[2]:
            copy.wait_recv()
        acc = xr_f[0, 0:128, :]
        for k in range(1, NX):
            acc = acc * decay(1, k) + xr_f[k, 0:128, :]
        total_f[...] = acc
        for j in range(NZ):
            zs_f[j] = acc[8 * j : 8 * j + 8, :]

    def forward_z1():
        for copy in z1:
            pl.when(mz != NZ - 1)(copy.start)
        zr_f[mz] = zs_f[mz]

    early = mz < EARLY
    hand_on = remote(handed, enter, hand_s, hand_r, at_z(1))

    def hand_over_state():
        plane = decay(1, 0) * decay(1, 1) * decay(1, 2) * decay(1, 3)
        handed[...] = enter[...] * plane + total_f[...]
        hand_on.start()

    def forward_x2():
        carry = enter[...]
        for k in range(NX):
            ws_f[k] = carry
            if k < NX - 1:
                carry = carry * decay(1, k) + xr_f[k, 0:128, :]
        for t, copy in x2_out[2]:
            pl.when(mx != t)(copy.start)
        inc[mx] = ws_f[mx]

    def backward_x2(h):
        part, rows_in = slice(64 * h, 64 * h + 64), slice(8 + 64 * h, 72 + 64 * h)
        carry = leave[part, :]
        for k in range(NX - 1, -1, -1):
            ws_b[k, part, :] = carry
            if k > 0:
                carry = carry * decay(0, k) + xr_b[k, rows_in, :]
        for t, copy in x2_out[h]:
            pl.when(mx != t)(copy.start)
        fol[mx, part, :] = ws_b[mx, part, :]

    def last(i):
        carried, map2, w_h, w_l, weight, acc_ref, hbm = (
            (fol, b2, xe_h, xe_l, end_w, gv_acc, gv_hbm),
            (inc, c2, gf_h, gf_l, from_w, out_acc, out_hbm),
        )[i]
        grad = local_maps[i]
        states = []
        for d in (0, 1, 3, 2):
            if d > 0:
                for copies in (x2[:2], x2[2:])[i]:
                    copies[FAR_X.index(d)].wait_recv()
            q = lax.rem(mx + NX - d, NX)
            state2 = split(carried[q])
            states.append((q, state2))
            grad = grad + dot3((w_h[q], w_l[q]), state2, NT)
        for k in range(NH):
            rs_s[i, k] = grad[16 * k : 16 * k + 16, :]
        for t in (1, 0, 3, 2, 5, 7, 4, 6):
            n = lax.min(lax.rem(t + 2 * NH - 1 - head, NH), NH - 2)
            copy = remote(rs_s.at[i, t], rs_r.at[i, head], rs_ss.at[i, n], rs_rs.at[i, n], (ctx, t))
            pl.when(head != t)(copy.start)
        own_piece(i).start()
        for n, (q, state2) in enumerate(states):
            acc_ref[q] = acc_ref[q] + weight[q] * dot3(map2, state2)
            store(i, n, acc_ref.at[q], hbm, q).start()

    def own_piece(i):
        return pltpu.make_async_copy(rs_s.at[i, head], rs_r.at[i, head], out_sem.at[i, NX])

    def store(i, n, src, hbm, q):
        return pltpu.make_async_copy(src, hbm.at[:, pl.ds(pl.multiple_of(q * 128, 128), 128)], out_sem.at[i, n])

    @pl.when(mz == 0)
    def _():
        forward_total()
        enter[...] = jnp.zeros((128, 128), F32)
        hand_over_state()
        pl.semaphore_wait(reach, 2)
        forward_z1()
        for copy in x1[0] + x1[1]:
            copy.wait_recv()
        forward_x2()

    @pl.when(mz != 0)
    def _():
        backward_z1()
        forward_total()
        pl.when(mz == 1)(hand_on.wait_recv)
        pl.when(mz == 1)(hand_over_state)
        forward_z1()
        pl.when(mz == 1)(forward_x2)

    scores, scores_t = dot3(c2, b2, NT), dot3(b2, c2, NT)
    inner = jnp.zeros((128, 128), F32)
    for q in range(NX):
        cols = slice(q * 128, (q + 1) * 128)
        x, gq = scaled[q], g[:, cols]
        xv, gv2 = split(x), split(gq)
        outs, grads = [], []
        for k in range(2):
            h = 2 * q + k
            mine = first if k == 0 else jnp.logical_not(first)
            gap = column(3, h) - cum[h : h + 1, :]
            kept = jnp.exp(jnp.where(lower, gap, -gap))
            below = jnp.where(lower, kept, 0.0)
            above = jnp.where(upper, kept, 0.0)
            part = split(jnp.where(mine, gq, 0.0))
            inner = inner + dot3(part, xv, NT) * below
            outs.append(dot3(split(scores * below), xv))
            grads.append(dot3(split(scores_t * above), gv2))
        skip = jnp.where(first[0:1], gain[2 * q], gain[2 * q + 1])
        step_w = pair(0, q)
        out_acc[q] = jnp.where(first, outs[0], outs[1]) + skip * v[:, cols]
        gv_acc[q] = step_w * jnp.where(first, grads[0], grads[1]) + skip * gq
    local_maps[1] = dot3(split(inner), b2)
    local_maps[0] = dot3(split(inner.T), c2)

    for h in range(2):
        for d, copy in z1b_in[h]:
            pl.when(jnp.logical_and(d != 0, lax.rem(mz + NZ - d, NZ) != 0))(copy.wait_recv)
    carry = jnp.zeros((8, 128), F32)
    for j in range(NZ - 1, -1, -1):
        ys_b[j] = carry
        if j > 0:
            carry = carry * zr_b[j, 8:9, :] + zr_b[j, 0:8, :]
    for t in (0, 1, 2, 3, 4, 5, 6, 7, 15, 14, 13, 12, 8, 11, 10, 9):
        n = lax.min(lax.rem(t + 2 * NZ - 1 - mz, NZ), NZ - 2)
        copy = remote(ys_b.at[t], leave.at[back_rows], z2_s.at[0, n], z2_r.at[0, n], (t * NX + mx, head))
        pl.when(mz != t)(copy.start)
    leave[back_rows, :] = ys_b[mz]

    @pl.when(mz == 2)
    def _():
        hand_on.wait_recv()
        if EARLY > 3:
            hand_over_state()
        forward_x2()

    for copy, d in zip(z1, FAR_Z):
        pl.when(lax.rem(mz + NZ - d, NZ) != NZ - 1)(copy.wait_recv)
    carry = zr_f[0]
    for j in range(1, NZ):
        ys_f[j] = carry
        if j < NZ - 1:
            carry = carry * zr_b[j, 8:9, :] + zr_f[j]
    for copy, d in zip(z2, FAR_Z):
        pl.when(lax.rem(mz + d, NZ) >= EARLY)(copy.start)

    if EARLY > 3:

        @pl.when(mz == 3)
        def _():
            hand_on.wait_recv()
            forward_x2()

    for h in range(2):
        for d, copy in z2b_in[h][:-1]:
            copy.wait_recv()
        d, copy = z2b_in[h][-1]
        pl.when(d != 0)(copy.wait_recv)
        backward_x2(h)

    @pl.when(early)
    def _():
        last(1)

    @pl.when(jnp.logical_not(early))
    def _():
        enter[mine_rows, :] = ys_f[mz]
        for copy in z2:
            copy.wait_recv()
        forward_x2()

    last(0)

    @pl.when(jnp.logical_not(early))
    def _():
        last(1)

    for h in range(2):
        for d, copy in z1b[h]:
            pl.when(jnp.logical_and(mz != 0, d != 0))(copy.wait_send)
    for copy in z1:
        pl.when(mz != NZ - 1)(copy.wait_send)
    for copy in sum(x1 + x2, []) + z2b:
        copy.wait_send()
    for copy, d in zip(z2, FAR_Z):
        pl.when(lax.rem(mz + d, NZ) >= EARLY)(copy.wait_send)
    pl.when(mz < EARLY - 1)(hand_on.wait_send)
    for i, (acc_ref, hbm) in enumerate(((gv_acc, gv_hbm), (out_acc, out_hbm))):
        for n in range(NX):
            store(i, n, acc_ref.at[n], hbm, n).wait()
        own_piece(i).wait()
    for i in (1, 0):
        for copy in rs[i]:
            copy.wait_send()
    for i in (1, 0):
        for copy in rs[i]:
            copy.wait_recv()


def hand_kernel(out_in, gv_in, pieces_in, out, gv, gi, go, wide, pieces, sums, sem):
    loads = [
        pltpu.make_async_copy(src, via, sem.at[0, i])
        for i, (src, via) in enumerate(((pieces_in, pieces), (out_in, wide.at[0]), (gv_in, wide.at[1])))
    ]
    stores = [
        pltpu.make_async_copy(via, dst, sem.at[1, i])
        for i, (via, dst) in enumerate(((sums.at[0], gi), (sums.at[1], go), (wide.at[0], out), (wide.at[1], gv)))
    ]
    for copy in loads:
        copy.start()
    loads[0].wait()
    for i in range(2):
        whole = pieces[i, 0]
        for k in range(1, NH):
            whole = whole + pieces[i, k]
        sums[i] = whole
        stores[i].start()
    for i in range(2):
        loads[i + 1].wait()
        stores[i + 2].start()
    for copy in stores:
        copy.wait()


def shards(values, step_size, decay_rate, input_map, output_map, skip_gain, grad_output):
    far = pl.BlockSpec(memory_space=pltpu.HBM)
    vmem = lambda *shape, dtype=F32: pltpu.VMEM(shape, dtype)
    dma = lambda *shape: pltpu.SemaphoreType.DMA(shape)
    full = jax.ShapeDtypeStruct(values.shape, F32)
    out, gv, pieces = pl.pallas_call(
        core_kernel,
        name="scan_core",
        out_shape=(full, full, jax.ShapeDtypeStruct((2, NH, 16, 128), F32)),
        in_specs=[far] * 7,
        out_specs=(far,) * 3,
        scratch_shapes=[
            vmem(128, 512), vmem(128, 512), vmem(8, 128), vmem(128, 128), vmem(128, 128),
            pltpu.SMEM((8,), F32), pltpu.SMEM((8,), F32),
            vmem(4, 128, 128), vmem(4, 128, 128), vmem(4, 128, 128), vmem(4, 128, 128),
            vmem(4, 128, 128, dtype=BF16), vmem(4, 128, 128, dtype=BF16),
            vmem(4, 128, 128, dtype=BF16), vmem(4, 128, 128, dtype=BF16), vmem(2, 128, 128),
            vmem(4, 129, 128), vmem(4, 136, 128), vmem(4, 129, 128), vmem(4, 136, 128),
            vmem(16, 8, 128), vmem(16, 9, 128), vmem(16, 8, 128), vmem(16, 9, 128),
            vmem(16, 8, 128), vmem(16, 8, 128), vmem(128, 128), vmem(128, 128), vmem(128, 128), vmem(128, 128),
            vmem(4, 128, 128), vmem(4, 128, 128), vmem(4, 128, 128), vmem(4, 128, 128),
            vmem(2, 8, 16, 128),
            pltpu.SemaphoreType.REGULAR, pltpu.SemaphoreType.DMA, pltpu.SemaphoreType.DMA, dma(7), dma(3, 3), dma(3, 3), dma(2, 15), dma(2, 15), dma(2, 15), dma(2, 15), dma(3, 3), dma(3, 3),
            dma(2, 7), dma(2, 7), dma(2, 5),
        ],
        compiler_params=pltpu.CompilerParams(
            collective_id=0, has_side_effects=True, vmem_limit_bytes=60 * 1024 * 1024
        ),
    )(values, step_size, decay_rate, input_map, output_map, skip_gain, grad_output)
    piece = jax.ShapeDtypeStruct((16, 128), F32)
    return pl.pallas_call(
        hand_kernel,
        name="hand_over",
        out_shape=(full, full, piece, piece),
        in_specs=[far] * 3,
        out_specs=(far,) * 4,
        scratch_shapes=[vmem(2, 128, 512), vmem(2, 8, 16, 128), vmem(2, 16, 128), dma(2, 4)],
    )(out, gv, pieces)


def solution(mesh):
    placed = (
        P("ctx", "head"),
        P("head", "ctx"),
        P("head"),
        P("ctx", None),
        P("ctx", None),
        P("head"),
        P("ctx", "head"),
    )
    return jax.shard_map(
        shards,
        mesh=mesh,
        in_specs=placed,
        out_specs=(
            P("ctx", "head"),
            P("ctx", "head"),
            P(("ctx", "head"), None),
            P(("ctx", "head"), None),
        ),
        check_vma=False,
    )
```
